32 devices in a mesh: groups: 2 (over x), ep: 4 (over y, core), sub: 4 (over z).
Axes of the slice: x: 2, y: 2, z: 4, core: 2. Of those that a mesh axis runs over, the one named last changes fastest.
Arguments:
- tokens: bfloat16 [256, 7168], P(('groups', 'ep', 'sub')), parts along dimension 0, may hold values from -6 to 6
- routes: int32 [256, 2], P(('groups', 'ep', 'sub')), parts along dimension 0, may hold values from 0 to 3, as said below
- gates: bfloat16 [256, 2], P(('groups', 'ep', 'sub')), parts along dimension 0, may hold values from 0.099609375 to 1
- expert_up: bfloat16 [4, 7168, 2, 1024], P('ep', None, None, 'sub'), may hold values from -0.0625 to 0.0625
- expert_down: bfloat16 [4, 1024, 7168], P('ep', 'sub'), may hold values from -0.1875 to 0.1875
- shared_up: bfloat16 [7168, 2, 2048], P(None, None, 'ep'), may hold values from -0.0625 to 0.0625
- shared_down: bfloat16 [2048, 7168], P('ep'), may hold values from -0.125 to 0.125
Outputs:
- mixed: bfloat16 [256, 7168], P(('groups', 'ep', 'sub')), parts along dimension 0
The draws below stay inside these ranges and needn't reach their ends.
There are 2 independent parts, one for each index of `groups`. The reference program is written for one: setup_inputs(seed, part) draws one part's arguments, and reference() takes and returns one part's arrays. A program takes and returns all parts, laid end to end along the dimension named above; an argument that names none is the same for every part. Nothing has to cross between parts.
Inputs may be any that keep to these rules, and one draw needn't show every extreme that they name: `routes`: each row names 2 different experts. The rows of one device name one expert at most 6 times; one expert is named exactly 6 times by the rows of every device, and the other experts share the remaining 2 * 8 - 6 names of a device as evenly as possible.
All inputs are finite; a program needn't handle non-finite values.
Results may differ from the reference program's by a relative error of at most 0.015.
Values may be sent and summed in bfloat16 or wider, within the bound.
No kernel may reach another device: no remote copies, remote signals or barrier semaphores. Data moves between devices by JAX's collectives and lax.ppermute only.
A program may use at most 128 MiB of HBM per device.

```python
import math
import jax
import jax.numpy as jnp
from jax import lax

D = 7168
FF = 1024
SFF = 2048
QBLOCK = 128
TOK_DEV = 8
TOPK = 2
EXPERTS = 4
CAP = 6
TOKENS = 128
N_EP = 4
N_SUB = 4


def draw_routes(key, part):
    key = jax.random.fold_in(key, 11)
    busiest = jax.random.randint(jax.random.fold_in(key, 1), (), 0, EXPERTS).astype(jnp.int32)
    block_count = TOKENS // TOK_DEV
    columns = jnp.arange(TOPK, dtype=jnp.int32)

    def one_block(position):
        block_key = jax.random.fold_in(key, position + 2)
        key_tok, key_other, key_shift = jax.random.split(block_key, 3)
        tok_perm = jax.random.permutation(key_tok, TOK_DEV).astype(jnp.int32)
        holders = (tok_perm < CAP).astype(jnp.int32)
        needed = TOPK - holders
        start_pos = jnp.cumsum(needed) - needed
        others = jax.random.permutation(key_other, EXPERTS - 1).astype(jnp.int32)
        others = others + (others >= busiest).astype(jnp.int32)
        spot = (start_pos[:, None] + columns[None, :] - holders[:, None]) % (EXPERTS - 1)
        picked = others[spot]
        picked = jnp.where((holders[:, None] == 1) & (columns[None, :] == 0), busiest, picked)
        shifts = jax.random.randint(key_shift, (TOK_DEV, 1), 0, TOPK).astype(jnp.int32)
        rotated = (columns[None, :] + shifts) % TOPK
        return jnp.take_along_axis(picked, rotated, axis=1)
    drawn = jax.vmap(one_block)(jnp.arange(block_count, dtype=jnp.int32))
    return drawn.reshape(TOKENS, TOPK).astype(jnp.int32)


def steps_of(own_key, extent, pieces, least, high):
    gain, own = 1.0, jax.random.fold_in(own_key, 6)
    for axis_at, blocks in pieces:
        steps = jnp.exp(jax.random.uniform(jax.random.fold_in(own, axis_at), (blocks,), jnp.float32, least / len(pieces), high / len(pieces)))
        gain = gain * jnp.repeat(steps, extent[axis_at] // blocks).reshape([-1 if axis == axis_at else 1 for axis in range(len(extent))])
    return gain


def centred(rng, shape, scale, reach, cuts=(), kind=jnp.bfloat16):
    values = jax.random.normal(rng, shape, jnp.float32) * scale
    if len(cuts) > 0:
        values = steps_of(rng, shape, cuts, -0.22, 0.18) * values
    return jnp.clip(values, min=-reach, max=reach).astype(kind)


def setup_inputs(seed: int = 0, part: int = 0) -> dict:
    seeds = jax.random.split(jax.random.key(seed), 8)
    part_keys = jax.random.split(jax.random.fold_in(seeds[7], part), 8)
    tokens = centred(part_keys[0], (TOKENS, D), 1.0, 6.0, ((0, 16),))
    routes = draw_routes(jax.random.fold_in(jax.random.fold_in(seeds[7], part), 71), part)
    gates = jnp.clip(jnp.exp(math.log(1.0) - 2.306499 * jax.random.uniform(part_keys[2], (TOKENS, TOPK), jnp.float32) ** steps_of(part_keys[2], (TOKENS, TOPK), ((0, 16),), -0.2, 0.2)), 0.099609375, 1.0).astype(jnp.bfloat16)
    expert_up = centred(seeds[3], (EXPERTS, D, 2, FF), D ** -0.5, 0.0625, ((0, 4), (3, 4)))
    expert_down = centred(seeds[4], (EXPERTS, FF, D), FF ** -0.5, 0.1875, ((0, 4), (1, 4)))
    shared_up = centred(seeds[5], (D, 2, SFF), D ** -0.5, 0.0625, ((2, 4),))
    shared_down = centred(seeds[6], (SFF, D), SFF ** -0.5, 0.125, ((0, 4),))
    return {"tokens": tokens, "routes": routes, "gates": gates, "expert_up": expert_up, "expert_down": expert_down, "shared_up": shared_up, "shared_down": shared_down}


def rounded_term(left, right):
    partial_value = jnp.dot(left, right, preferred_element_type=jnp.float32).astype(jnp.bfloat16)
    return lax.optimization_barrier(partial_value).astype(jnp.float32)


def block_restore(rows):
    count, width = rows.shape
    blocks = rows.astype(jnp.float32).reshape(count, width // QBLOCK, QBLOCK)
    largest = jnp.max(jnp.abs(blocks), axis=2)
    scale = ((largest + 1e-6) / 448.0).astype(jnp.bfloat16).astype(jnp.float32)
    scaled = (blocks / scale[:, :, None]).astype(jnp.bfloat16)
    scaled = lax.optimization_barrier(scaled).astype(jnp.float32)
    return (scaled * scale[:, :, None]).astype(jnp.bfloat16).reshape(count, width)


def reference(tokens, routes, gates, expert_up, expert_down, shared_up, shared_down):
    shared_gate = jnp.dot(tokens, shared_up[:, 0, :], preferred_element_type=jnp.float32)
    shared_lift = jnp.dot(tokens, shared_up[:, 1, :], preferred_element_type=jnp.float32)
    shared_hidden = (jax.nn.silu(shared_gate) * shared_lift).astype(jnp.bfloat16)
    shared_group = SFF // N_EP

    def shared_step(running, position):
        hidden_part = lax.dynamic_slice_in_dim(shared_hidden, position * shared_group, shared_group, 1)
        down_part = lax.dynamic_slice_in_dim(shared_down, position * shared_group, shared_group, 0)
        return running + rounded_term(hidden_part, down_part), None

    running = jnp.zeros((TOKENS, D), jnp.float32)
    running, _ = lax.scan(shared_step, running, jnp.arange(N_EP, dtype=jnp.int32))

    restored = block_restore(tokens)
    row_limit = N_EP * N_SUB * CAP
    sub_group = FF // N_SUB
    gate_values = gates.astype(jnp.float32)

    def expert_step(running, expert):
        chosen = routes == expert
        named_any = jnp.any(chosen, axis=1)
        weight = jnp.sum(jnp.where(chosen, gate_values, 0.0), axis=1)
        picked = jnp.nonzero(named_any, size=row_limit, fill_value=0)[0].astype(jnp.int32)
        valid = jnp.arange(row_limit, dtype=jnp.int32) < jnp.sum(named_any.astype(jnp.int32))
        token_rows = restored[picked]
        up_weights = lax.dynamic_index_in_dim(expert_up, expert, 0, keepdims=False)
        down_weights = lax.dynamic_index_in_dim(expert_down, expert, 0, keepdims=False)
        gate_proj = jnp.dot(token_rows, up_weights[:, 0, :], preferred_element_type=jnp.float32)
        up_proj = jnp.dot(token_rows, up_weights[:, 1, :], preferred_element_type=jnp.float32)
        hidden = (jax.nn.silu(gate_proj) * up_proj).astype(jnp.bfloat16)

        def group_step(accum, position):
            hidden_part = lax.dynamic_slice_in_dim(hidden, position * sub_group, sub_group, 1)
            down_part = lax.dynamic_slice_in_dim(down_weights, position * sub_group, sub_group, 0)
            return accum + rounded_term(hidden_part, down_part), None

        expert_out = jnp.zeros((row_limit, D), jnp.float32)
        expert_out, _ = lax.scan(group_step, expert_out, jnp.arange(N_SUB, dtype=jnp.int32))
        weighted = (weight[picked][:, None] * expert_out).astype(jnp.bfloat16)
        weighted = lax.optimization_barrier(weighted).astype(jnp.float32)
        weighted = jnp.where(valid[:, None], weighted, jnp.float32(0.0))
        return running.at[picked].add(weighted), None

    running, _ = lax.scan(expert_step, running, jnp.arange(EXPERTS, dtype=jnp.int32))
    return running.astype(jnp.bfloat16)
```

```python
import jax
import jax.numpy as jnp
from jax import lax
from jax.sharding import PartitionSpec as P

QBLOCK = 128
LANES = 128
CORES = 2


def silu_product(projected):
    half_width = projected.shape[1] // 2
    return (jax.nn.silu(projected[:, :half_width]) * projected[:, half_width:]).astype(jnp.bfloat16)


def block_restored(rows):
    count, width = rows.shape
    blocks = rows.astype(jnp.float32).reshape(count, width // QBLOCK, QBLOCK)
    largest = jnp.max(jnp.abs(blocks), axis=2)
    scale = ((largest + 1e-06) / 448.0).astype(jnp.bfloat16).astype(jnp.float32)[:, :, None]
    scaled = (blocks / scale).astype(jnp.bfloat16).astype(jnp.float32)
    return (scaled * scale).astype(jnp.bfloat16).reshape(count, width)


def exchange(rows, axis, flip):
    size = lax.axis_size(axis)
    return lax.ppermute(rows, axis, [(i, i ^ flip) for i in range(size)])


def gathered_ep(rows, experts):
    parts = [rows] + [exchange(rows, "ep", chip) for chip in range(CORES, experts, CORES)]
    half = jnp.concatenate(parts, axis=0)
    return jnp.concatenate([half, exchange(half, "ep", 1)], axis=0)


def summed_ep(partial, experts):
    half = partial.shape[0] // CORES
    other = exchange(partial[half:], "ep", 1)
    pair = (partial[:half].astype(jnp.float32) + other.astype(jnp.float32)).astype(jnp.bfloat16)
    count = half * CORES // experts
    total = pair[:count].astype(jnp.float32)
    for chip in range(CORES, experts, CORES):
        at = chip // CORES * count
        total = total + exchange(pair[at:at + count], "ep", chip).astype(jnp.float32)
    return total


def per_device(tokens, routes, gates, expert_up, expert_down, shared_up, shared_down):
    count, width = tokens.shape
    experts = lax.axis_size("ep")
    subs = lax.axis_size("sub")
    me = lax.axis_index("ep")
    bf = jnp.bfloat16

    lanes = -(-experts // LANES) * LANES
    chosen = routes[:, :, None] == jnp.arange(lanes, dtype=jnp.int32)
    weight = jnp.sum(jnp.where(chosen, gates[:, :, None], jnp.zeros((), bf)), axis=1)
    routed_rows = jnp.concatenate([block_restored(tokens), weight.astype(bf)], axis=1)
    own = jnp.concatenate([tokens, routed_rows], axis=1)

    far = [exchange(routed_rows, "sub", k) for k in range(subs - 1, 0, -1)]
    own_all = gathered_ep(own, experts)
    far_all = gathered_ep(jnp.concatenate(far, axis=0), experts)

    shared_weights = shared_up.reshape(width, -1)
    expert_weights = expert_up.reshape(width, -1)
    down_weights = expert_down.reshape(-1, width)

    def routed(rows):
        hidden = silu_product(jnp.dot(rows[:, :width], expert_weights, preferred_element_type=jnp.float32))
        out = jnp.dot(hidden, down_weights, preferred_element_type=jnp.float32)
        named = jnp.arange(lanes, dtype=jnp.int32) == me
        gate = jnp.sum(jnp.where(named, rows[:, width:].astype(jnp.float32), 0.0), axis=1)
        return gate[:, None] * out

    shared_hidden = silu_product(jnp.dot(own_all[:, :width], shared_weights, preferred_element_type=jnp.float32))
    own_part = jnp.dot(shared_hidden, shared_down, preferred_element_type=jnp.float32)
    own_part = (own_part + routed(own_all[:, width:])).astype(bf)
    far_part = routed(far_all).astype(bf)

    total = summed_ep(own_part, experts)
    far_sum = summed_ep(far_part, experts).astype(bf)
    for at, k in enumerate(range(subs - 1, 0, -1)):
        total = total + exchange(far_sum[at * count:(at + 1) * count], "sub", k).astype(jnp.float32)
    return total.astype(bf)


def solution(mesh):
    return jax.shard_map(
        per_device,
        mesh=mesh,
        in_specs=(
            P(("groups", "ep", "sub"), None),
            P(("groups", "ep", "sub"), None),
            P(("groups", "ep", "sub"), None),
            P("ep", None, None, "sub"),
            P("ep", "sub", None),
            P(None, None, "ep"),
            P("ep", None),
        ),
        out_specs=P(("groups", "ep", "sub"), None),
        check_vma=False,
    )
```

```python
import jax
import jax.numpy as jnp
from jax import lax
from jax.experimental import pallas as pl
from jax.experimental.pallas import tpu as pltpu
from jax.sharding import PartitionSpec as P

QBLOCK = 128
LANES = 128
CORES = 2


def silu_product(projected):
    half_width = projected.shape[1] // 2
    return (jax.nn.silu(projected[:, :half_width]) * projected[:, half_width:]).astype(jnp.bfloat16)


def owner_kernel(tokens_ref, routes_ref, gates_ref, ready_ref, routed_ref, tokens, routes, gates, sems):
    del ready_ref
    copies = [
        pltpu.make_async_copy(source, target, sems.at[i])
        for i, (source, target) in enumerate(
            ((tokens_ref, tokens), (routes_ref, routes), (gates_ref, gates))
        )
    ]
    for copy in copies:
        copy.start()
    for copy in copies:
        copy.wait()
    count, width = tokens.shape
    for at in range(0, width, QBLOCK):
        block = tokens[:, at:at + QBLOCK].astype(jnp.float32)
        largest = jnp.max(jnp.abs(block), axis=1, keepdims=True)
        scale = ((largest + 1e-06) / 448.0).astype(jnp.bfloat16).astype(jnp.float32)
        scaled = (block / scale).astype(jnp.bfloat16).astype(jnp.float32)
        routed_ref[:, at:at + QBLOCK] = (scaled * scale).astype(jnp.bfloat16)
    lanes = routed_ref.shape[1] - width
    expert = lax.broadcasted_iota(jnp.int32, (count, lanes), 1)
    diagonal = (
        lax.broadcasted_iota(jnp.int32, (count, count), 0)
        == lax.broadcasted_iota(jnp.int32, (count, count), 1)
    )

    def column(row):
        return jnp.sum(jnp.where(diagonal, row, 0), axis=1, keepdims=True)

    weight = jnp.zeros((count, lanes), jnp.float32)
    for k in range(routes.shape[0]):
        gate = column(gates[k:k + 1, :].astype(jnp.float32))
        named = column(routes[k:k + 1, :])
        weight = weight + jnp.where(named == expert, gate, 0.0)
    routed_ref[:, width:] = weight.astype(jnp.bfloat16)


def owner_rows(tokens, routes, gates, ready, lanes):
    count, width = tokens.shape
    operands = (tokens, routes.T, gates.T)
    return pl.pallas_call(
        owner_kernel,
        in_specs=[pl.BlockSpec(memory_space=pltpu.HBM)] * 3 + [pl.BlockSpec(memory_space=pl.ANY)],
        out_specs=pl.BlockSpec(memory_space=pltpu.VMEM),
        out_shape=jax.ShapeDtypeStruct((count, width + lanes), tokens.dtype),
        scratch_shapes=[pltpu.VMEM(x.shape, x.dtype) for x in operands]
        + [pltpu.SemaphoreType.DMA((len(operands),))],
        compiler_params=pltpu.CompilerParams(vmem_limit_bytes=4 << 20),
    )(*(pltpu.with_memory_space_constraint(x, pltpu.HBM) for x in operands), ready)


def split_kernel(pair_ref, ready_ref, flat_ref, raw, sems):
    del ready_ref
    step, steps = pl.program_id(0), pl.num_programs(0)
    block, hidden = flat_ref.shape[0], pair_ref.shape[2]

    def fetch(i):
        rows = pl.ds(i * block, block)
        return pltpu.make_async_copy(pair_ref.at[rows], raw.at[rows], sems.at[i])

    @pl.when(step == 0)
    def _():
        for i in range(sems.shape[0]):
            fetch(i).start()

    fetch(step).wait()
    both = jnp.swapaxes(raw[pl.ds(step * block, block)], 0, 1)
    flat_ref[:, :hidden] = both[0]
    flat_ref[:, hidden:] = both[1]


def flat_pairs(pairs, ready, steps):
    depth, _, hidden = pairs.shape
    block = depth // steps
    return pl.pallas_call(
        split_kernel,
        grid=(steps,),
        in_specs=[pl.BlockSpec(memory_space=pltpu.HBM), pl.BlockSpec(memory_space=pl.ANY)],
        out_specs=pl.BlockSpec((block, 2 * hidden), lambda i: (i, 0)),
        out_shape=jax.ShapeDtypeStruct((depth, 2 * hidden), pairs.dtype),
        scratch_shapes=[pltpu.VMEM(pairs.shape, pairs.dtype), pltpu.SemaphoreType.DMA((steps,))],
        compiler_params=pltpu.CompilerParams(vmem_limit_bytes=16 << 20),
        cost_estimate=pl.CostEstimate(
            flops=0, bytes_accessed=8 * depth * hidden, transcendentals=0
        ),
    )(pltpu.with_memory_space_constraint(pairs, pltpu.HBM), ready)


def shared_up_kernel(rows_ref, up_ref, ready_ref, middle_ref, up, sums, sems):
    del ready_ref
    steps = sems.shape[0]
    block = up.shape[0] // steps

    def fetch(i):
        at = pl.ds(i * block, block)
        return pltpu.make_async_copy(up_ref.at[at], up.at[at], sems.at[i])

    for i in range(steps):
        fetch(i).start()
    for i in range(steps):
        fetch(i).wait()
        both = jnp.swapaxes(up[i * block:(i + 1) * block], 0, 1)
        left = rows_ref[:, i * block:(i + 1) * block]
        for half in range(2):
            term = jnp.dot(left, both[half], preferred_element_type=jnp.float32)
            sums[half] = term if i == 0 else sums[half] + term
    gate, lift = sums[0], sums[1]
    middle_ref[...] = (gate / (1.0 + jnp.exp(-gate)) * lift).astype(jnp.bfloat16)


def shared_middle(rows, up, ready):
    count, (width, _, hidden) = rows.shape[0], up.shape
    steps = 7
    return pl.pallas_call(
        shared_up_kernel,
        in_specs=[
            pl.BlockSpec(memory_space=pltpu.VMEM),
            pl.BlockSpec(memory_space=pltpu.HBM),
            pl.BlockSpec(memory_space=pl.ANY),
        ],
        out_specs=pl.BlockSpec(memory_space=pltpu.VMEM),
        out_shape=jax.ShapeDtypeStruct((count, hidden), jnp.bfloat16),
        scratch_shapes=[
            pltpu.VMEM(up.shape, up.dtype),
            pltpu.VMEM((2, count, hidden), jnp.float32),
            pltpu.SemaphoreType.DMA((steps,)),
        ],
        compiler_params=pltpu.CompilerParams(vmem_limit_bytes=20 << 20),
        cost_estimate=pl.CostEstimate(
            flops=4 * count * hidden * width,
            bytes_accessed=4 * hidden * width,
            transcendentals=0,
        ),
    )(rows, pltpu.with_memory_space_constraint(up, pltpu.HBM), ready)


def after(value, ready):
    return lax.optimization_barrier((value, ready))[0]


def exchange(rows, axis, flip):
    size = lax.axis_size(axis)
    return lax.ppermute(rows, axis, [(i, i ^ flip) for i in range(size)])


def half_ep(rows, experts):
    parts = [exchange(rows, "ep", chip) for chip in range(CORES, experts, CORES)]
    return jnp.concatenate([rows] + parts, axis=0)


def summed_ep(partial, experts):
    half = partial.shape[0] // CORES
    other = exchange(partial[half:], "ep", 1)
    pair = (partial[:half].astype(jnp.float32) + other.astype(jnp.float32)).astype(jnp.bfloat16)
    count = half * CORES // experts
    total = pair[:count].astype(jnp.float32)
    for chip in range(CORES, experts, CORES):
        at = chip // CORES * count
        total = total + exchange(pair[at:at + count], "ep", chip).astype(jnp.float32)
    return total


def per_device(tokens, routes, gates, expert_up, expert_down, shared_up, shared_down):
    count, width = tokens.shape
    experts = lax.axis_size("ep")
    subs = lax.axis_size("sub")
    me = lax.axis_index("ep")
    bf = jnp.bfloat16

    lanes = -(-experts // LANES) * LANES
    named = (jnp.arange(lanes, dtype=jnp.int32) == me).astype(jnp.float32)
    token_half = half_ep(tokens, experts)
    routed_rows = owner_rows(tokens, routes, gates, named, lanes)

    groups = [[subs // 2], [k for k in range(subs - 1, 0, -1) if k != subs // 2]]
    order = [k for group in groups for k in group]
    far = jnp.concatenate([exchange(routed_rows, "sub", k) for k in order], axis=0)
    own_half = half_ep(routed_rows, experts)
    token_all = jnp.concatenate([token_half, exchange(token_half, "ep", 1)], axis=0)
    expert_weights = flat_pairs(expert_up[0], routed_rows, 4)
    far, expert_weights = lax.optimization_barrier((far, expert_weights))
    middle = shared_middle(token_all, shared_up, far)

    far_half = half_ep(far, experts)
    half = after(jnp.concatenate([own_half, far_half], axis=0), middle)
    other = exchange(half, "ep", 1)
    rows = jnp.concatenate([half, other], axis=0)
    hidden = silu_product(jnp.dot(rows[:, :width], expert_weights, preferred_element_type=jnp.float32))
    gate = jnp.sum(named * rows[:, width:].astype(jnp.float32), axis=1)
    down_weights = expert_down.reshape(-1, width)

    hidden = hidden.reshape(CORES, half.shape[0], -1)
    gate = gate.reshape(CORES, half.shape[0])

    def routed(first, last):
        out = jnp.dot(hidden[:, first:last].reshape(CORES * (last - first), -1), down_weights, preferred_element_type=jnp.float32)
        return gate[:, first:last].reshape(-1, 1) * out

    split = own_half.shape[0]
    far_part = routed(split, half.shape[0]).astype(bf).reshape(experts, len(order), count, width)
    sums, at = [], 0
    for group in groups:
        part = far_part[:, at:at + len(group)].reshape(-1, width)
        sums.append(summed_ep(part, experts).astype(bf))
        at += len(group)

    middle = after(middle, far_part)
    own_part = jnp.dot(middle, shared_down, preferred_element_type=jnp.float32)
    own_part = (own_part + routed(0, split)).astype(bf)
    total = summed_ep(own_part, experts)
    for rows, group in zip(sums, groups):
        for at, k in enumerate(group):
            total = total + exchange(rows[at * count:(at + 1) * count], "sub", k).astype(jnp.float32)
    return total.astype(bf)


def solution(mesh):
    return jax.shard_map(
        per_device,
        mesh=mesh,
        in_specs=(
            P(("groups", "ep", "sub"), None),
            P(("groups", "ep", "sub"), None),
            P(("groups", "ep", "sub"), None),
            P("ep", None, None, "sub"),
            P("ep", "sub", None),
            P(None, None, "ep"),
            P("ep", None),
        ),
        out_specs=P(("groups", "ep", "sub"), None),
        check_vma=False,
    )
```

```python
import functools

import jax
import jax.numpy as jnp
from jax import lax
from jax.experimental import pallas as pl
from jax.experimental.pallas import tpu as pltpu
from jax.sharding import PartitionSpec as P

QBLOCK = 128
LANES = 128
CORES = 2
VMEM_LIMIT = 30 << 20


def owner_kernel(tokens_ref, routes_ref, gates_ref, ready_ref, routed_ref, tokens, routes, gates, sems):
    del ready_ref
    copies = [
        pltpu.make_async_copy(source, target, sems.at[i])
        for i, (source, target) in enumerate(
            ((tokens_ref, tokens), (routes_ref, routes), (gates_ref, gates))
        )
    ]
    for copy in copies:
        copy.start()
    for copy in copies:
        copy.wait()
    count, width = tokens.shape
    for at in range(0, width, QBLOCK):
        block = tokens[:, at:at + QBLOCK].astype(jnp.float32)
        largest = jnp.max(jnp.abs(block), axis=1, keepdims=True)
        scale = ((largest + 1e-06) / 448.0).astype(jnp.bfloat16).astype(jnp.float32)
        scaled = (block / scale).astype(jnp.bfloat16).astype(jnp.float32)
        routed_ref[:, at:at + QBLOCK] = (scaled * scale).astype(jnp.bfloat16)
    lanes = routed_ref.shape[1] - width
    expert = lax.broadcasted_iota(jnp.int32, (count, lanes), 1)
    diagonal = (
        lax.broadcasted_iota(jnp.int32, (count, count), 0)
        == lax.broadcasted_iota(jnp.int32, (count, count), 1)
    )

    def column(row):
        return jnp.sum(jnp.where(diagonal, row, 0), axis=1, keepdims=True)

    weight = jnp.zeros((count, lanes), jnp.float32)
    for k in range(routes.shape[0]):
        gate = column(gates[k:k + 1, :].astype(jnp.float32))
        named = column(routes[k:k + 1, :])
        weight = weight + jnp.where(named == expert, gate, 0.0)
    routed_ref[:, width:] = weight.astype(jnp.bfloat16)


def owner_rows(tokens, routes, gates, ready, lanes):
    count, width = tokens.shape
    operands = (tokens, routes.T, gates.T)
    return pl.pallas_call(
        owner_kernel,
        in_specs=[pl.BlockSpec(memory_space=pltpu.HBM)] * 3 + [pl.BlockSpec(memory_space=pl.ANY)],
        out_specs=pl.BlockSpec(memory_space=pltpu.VMEM),
        out_shape=jax.ShapeDtypeStruct((count, width + lanes), tokens.dtype),
        scratch_shapes=[pltpu.VMEM(x.shape, x.dtype) for x in operands]
        + [pltpu.SemaphoreType.DMA((len(operands),))],
        compiler_params=pltpu.CompilerParams(vmem_limit_bytes=4 << 20),
    )(*(pltpu.with_memory_space_constraint(x, pltpu.HBM) for x in operands), ready)


def weights_kernel(pair_ref, down_ref, shared_ref, ready_ref, flat_ref, down_out, shared_out, raw, sems):
    del ready_ref
    steps = sems.shape[0] - 2
    block, hidden = raw.shape[0] // steps, pair_ref.shape[2]

    def fetch(i):
        rows = pl.ds(i * block, block)
        return pltpu.make_async_copy(pair_ref.at[rows], raw.at[rows], sems.at[i])

    downs = [
        pltpu.make_async_copy(down_ref, down_out, sems.at[steps]),
        pltpu.make_async_copy(shared_ref, shared_out, sems.at[steps + 1]),
    ]
    for i in range(steps):
        fetch(i).start()
    for copy in downs:
        copy.start()
    for i in range(steps):
        fetch(i).wait()
        at = slice(i * block, (i + 1) * block)
        both = jnp.swapaxes(raw[at], 0, 1)
        flat_ref[at, :hidden] = both[0]
        flat_ref[at, hidden:] = both[1]
    for copy in downs:
        copy.wait()


def held_weights(pairs, down, shared, ready):
    depth, _, hidden = pairs.shape
    steps = 4
    operands = [pltpu.with_memory_space_constraint(x, pltpu.HBM) for x in (pairs, down, shared)]
    return pl.pallas_call(
        weights_kernel,
        in_specs=[pl.BlockSpec(memory_space=pltpu.HBM)] * 3 + [pl.BlockSpec(memory_space=pl.ANY)],
        out_specs=[pl.BlockSpec(memory_space=pltpu.VMEM)] * 3,
        out_shape=(
            jax.ShapeDtypeStruct((depth, 2 * hidden), pairs.dtype),
            jax.ShapeDtypeStruct(down.shape, down.dtype),
            jax.ShapeDtypeStruct(shared.shape, shared.dtype),
        ),
        scratch_shapes=[pltpu.VMEM(pairs.shape, pairs.dtype), pltpu.SemaphoreType.DMA((steps + 2,))],
        compiler_params=pltpu.CompilerParams(vmem_limit_bytes=VMEM_LIMIT),
        cost_estimate=pl.CostEstimate(
            flops=0, bytes_accessed=8 * depth * hidden, transcendentals=0
        ),
    )(*operands, ready)


def shared_up_kernel(rows_ref, up_ref, ready_ref, middle_ref, up, sums, sems):
    del ready_ref
    steps = sems.shape[0]
    block = up.shape[0] // steps

    def fetch(i):
        at = pl.ds(i * block, block)
        return pltpu.make_async_copy(up_ref.at[at], up.at[at], sems.at[i])

    for i in range(steps):
        fetch(i).start()
    for i in range(steps):
        fetch(i).wait()
        both = jnp.swapaxes(up[i * block:(i + 1) * block], 0, 1)
        left = rows_ref[:, i * block:(i + 1) * block]
        for half in range(2):
            term = jnp.dot(left, both[half], preferred_element_type=jnp.float32)
            sums[half] = term if i == 0 else sums[half] + term
    gate, lift = sums[0], sums[1]
    middle_ref[...] = (gate / (1.0 + jnp.exp(-gate)) * lift).astype(jnp.bfloat16)


def shared_middle(rows, up, ready):
    count, (width, _, hidden) = rows.shape[0], up.shape
    steps = 7
    return pl.pallas_call(
        shared_up_kernel,
        in_specs=[
            pl.BlockSpec(memory_space=pltpu.VMEM),
            pl.BlockSpec(memory_space=pltpu.HBM),
            pl.BlockSpec(memory_space=pl.ANY),
        ],
        out_specs=pl.BlockSpec(memory_space=pltpu.VMEM),
        out_shape=jax.ShapeDtypeStruct((count, hidden), jnp.bfloat16),
        scratch_shapes=[
            pltpu.VMEM(up.shape, up.dtype),
            pltpu.VMEM((2, count, hidden), jnp.float32),
            pltpu.SemaphoreType.DMA((steps,)),
        ],
        compiler_params=pltpu.CompilerParams(vmem_limit_bytes=20 << 20),
        cost_estimate=pl.CostEstimate(
            flops=4 * count * hidden * width,
            bytes_accessed=4 * hidden * width,
            transcendentals=0,
        ),
    )(rows, pltpu.with_memory_space_constraint(up, pltpu.HBM), ready)


def routed_up_kernel(layout, half_ref, other_ref, flat_ref, named_ref, *rest):
    outs, sums = rest[:-1], rest[-1]
    depth, hidden = flat_ref.shape[0], flat_ref.shape[1] // 2
    steps = 7
    block = depth // steps
    for i in range(steps):
        at = slice(i * block, (i + 1) * block)
        left = jnp.concatenate([half_ref[:, at], other_ref[:, at]], axis=0)
        term = jnp.dot(left, flat_ref[at, :], preferred_element_type=jnp.float32)
        sums[...] = term if i == 0 else sums[...] + term
    weight = jnp.concatenate([half_ref[:, depth:], other_ref[:, depth:]], axis=0)
    named = weight.astype(jnp.float32) * named_ref[...]
    weight = jnp.sum(named, axis=1, keepdims=True)
    gate, lift = sums[:, :hidden], sums[:, hidden:]
    sums[:, :hidden] = gate / (1.0 + jnp.exp(-gate)) * lift * weight
    for out, pieces in zip(outs, layout):
        rows = [sums[first:first + count, :hidden] for first, count in pieces]
        out[...] = jnp.concatenate(rows, axis=0).astype(jnp.bfloat16)


def routed_hidden(half, other, flat, named, layout):
    count, hidden = 2 * half.shape[0], flat.shape[1] // 2
    return pl.pallas_call(
        functools.partial(routed_up_kernel, layout),
        in_specs=[pl.BlockSpec(memory_space=pltpu.VMEM)] * 4,
        out_specs=[pl.BlockSpec(memory_space=pltpu.VMEM)] * len(layout),
        out_shape=[
            jax.ShapeDtypeStruct((sum(rows for _, rows in pieces), hidden), jnp.bfloat16)
            for pieces in layout
        ],
        scratch_shapes=[pltpu.VMEM((count, 2 * hidden), jnp.float32)],
        compiler_params=pltpu.CompilerParams(vmem_limit_bytes=VMEM_LIMIT),
        cost_estimate=pl.CostEstimate(
            flops=2 * count * flat.size, bytes_accessed=2 * flat.size, transcendentals=0
        ),
    )(half, other, flat, named)


def after(value, ready):
    return lax.optimization_barrier((value, ready))[0]


def exchange(rows, axis, flip):
    size = lax.axis_size(axis)
    return lax.ppermute(rows, axis, [(i, i ^ flip) for i in range(size)])


def half_ep(rows, experts):
    parts = [exchange(rows, "ep", chip) for chip in range(CORES, experts, CORES)]
    return jnp.concatenate([rows] + parts, axis=0)


def pair_sum(partial):
    half = partial.shape[0] // CORES
    other = exchange(partial[half:], "ep", 1)
    return (partial[:half].astype(jnp.float32) + other.astype(jnp.float32)).astype(jnp.bfloat16)


def chip_sum(pair, experts):
    count = pair.shape[0] * CORES // experts
    total = pair[:count].astype(jnp.float32)
    for chip in range(CORES, experts, CORES):
        at = chip // CORES * count
        total = total + exchange(pair[at:at + count], "ep", chip).astype(jnp.float32)
    return total


def per_device(tokens, routes, gates, expert_up, expert_down, shared_up, shared_down):
    count, width = tokens.shape
    experts = lax.axis_size("ep")
    subs = lax.axis_size("sub")
    me = lax.axis_index("ep")
    bf = jnp.bfloat16

    lanes = -(-experts // LANES) * LANES
    named = (lax.broadcasted_iota(jnp.int32, (1, lanes), 1) == me).astype(jnp.float32)
    routed_rows = owner_rows(tokens, routes, gates, named, lanes)
    token_half = half_ep(after(tokens, routed_rows), experts)

    groups = [[subs // 2], [k for k in range(subs - 1, 0, -1) if k != subs // 2]]
    order = [k for group in groups for k in group]
    far = jnp.concatenate([exchange(routed_rows, "sub", k) for k in order], axis=0)
    own_half = half_ep(routed_rows, experts)
    token_all = jnp.concatenate([token_half, exchange(token_half, "ep", 1)], axis=0)
    expert_weights, down_weights, shared_weights = held_weights(
        expert_up[0], expert_down[0], shared_down, routed_rows
    )
    far, expert_weights = lax.optimization_barrier((far, expert_weights))
    middle = shared_middle(token_all, shared_up, far)

    far_half = half_ep(far, experts)
    half = after(jnp.concatenate([own_half, far_half], axis=0), middle)
    other = exchange(half, "ep", 1)

    chips, split = experts // CORES, own_half.shape[0]
    layout = [[(core * half.shape[0], split) for core in range(CORES)]]
    at = 0
    for group in groups:
        size = len(group) * count
        layout.append([
            (core * half.shape[0] + split + chip * len(order) * count + at, size)
            for core in range(CORES) for chip in range(chips)
        ])
        at += size
    own_hidden, *far_hidden = routed_hidden(half, other, expert_weights, named, layout)

    def down(hidden, weights):
        return jnp.dot(hidden, weights, preferred_element_type=jnp.float32)

    pairs = [pair_sum(down(hidden, down_weights).astype(bf)) for hidden in far_hidden]
    middle, own_hidden = after((middle, own_hidden), pairs[-1])
    own_part = (down(middle, shared_weights) + down(own_hidden, down_weights)).astype(bf)
    sums = [chip_sum(pair, experts).astype(bf) for pair in pairs]
    total = chip_sum(pair_sum(own_part), experts)
    for rows, group in zip(sums, groups):
        for at, k in enumerate(group):
            total = total + exchange(rows[at * count:(at + 1) * count], "sub", k).astype(jnp.float32)
    return total.astype(bf)


def solution(mesh):
    return jax.shard_map(
        per_device,
        mesh=mesh,
        in_specs=(
            P(("groups", "ep", "sub"), None),
            P(("groups", "ep", "sub"), None),
            P(("groups", "ep", "sub"), None),
            P("ep", None, None, "sub"),
            P("ep", "sub", None),
            P(None, None, "ep"),
            P("ep", None),
        ),
        out_specs=P(("groups", "ep", "sub"), None),
        check_vma=False,
    )
```

```python
import functools

import jax
import jax.numpy as jnp
from jax import lax
from jax.experimental import pallas as pl
from jax.experimental.pallas import tpu as pltpu
from jax.sharding import PartitionSpec as P

QBLOCK = 128
LANES = 128
CORES = 2
VMEM_LIMIT = 30 << 20


def owner_kernel(tokens_ref, routes_ref, gates_ref, ready_ref, routed_ref, tokens, routes, gates, sems):
    del ready_ref
    copies = [
        pltpu.make_async_copy(source, target, sems.at[i])
        for i, (source, target) in enumerate(
            ((tokens_ref, tokens), (routes_ref, routes), (gates_ref, gates))
        )
    ]
    for copy in copies:
        copy.start()
    for copy in copies:
        copy.wait()
    count, width = tokens.shape
    for at in range(0, width, QBLOCK):
        block = tokens[:, at:at + QBLOCK].astype(jnp.float32)
        largest = jnp.max(jnp.abs(block), axis=1, keepdims=True)
        scale = ((largest + 1e-06) / 448.0).astype(jnp.bfloat16).astype(jnp.float32)
        scaled = (block / scale).astype(jnp.bfloat16).astype(jnp.float32)
        routed_ref[:, at:at + QBLOCK] = (scaled * scale).astype(jnp.bfloat16)
    lanes = routed_ref.shape[1] - width
    expert = lax.broadcasted_iota(jnp.int32, (count, lanes), 1)
    diagonal = (
        lax.broadcasted_iota(jnp.int32, (count, count), 0)
        == lax.broadcasted_iota(jnp.int32, (count, count), 1)
    )

    def column(row):
        return jnp.sum(jnp.where(diagonal, row, 0), axis=1, keepdims=True)

    weight = jnp.zeros((count, lanes), jnp.float32)
    for k in range(routes.shape[0]):
        gate = column(gates[k:k + 1, :].astype(jnp.float32))
        named = column(routes[k:k + 1, :])
        weight = weight + jnp.where(named == expert, gate, 0.0)
    routed_ref[:, width:] = weight.astype(jnp.bfloat16)


def owner_rows(tokens, routes, gates, ready, lanes):
    count, width = tokens.shape
    operands = (tokens, routes.T, gates.T)
    return pl.pallas_call(
        owner_kernel,
        in_specs=[pl.BlockSpec(memory_space=pltpu.HBM)] * 3 + [pl.BlockSpec(memory_space=pl.ANY)],
        out_specs=pl.BlockSpec(memory_space=pltpu.VMEM),
        out_shape=jax.ShapeDtypeStruct((count, width + lanes), tokens.dtype),
        scratch_shapes=[pltpu.VMEM(x.shape, x.dtype) for x in operands]
        + [pltpu.SemaphoreType.DMA((len(operands),))],
        compiler_params=pltpu.CompilerParams(vmem_limit_bytes=4 << 20),
    )(*(pltpu.with_memory_space_constraint(x, pltpu.HBM) for x in operands), ready)


def weights_kernel(pair_ref, down_ref, shared_ref, ready_ref, flat_ref, down_out, shared_out, raw, sems):
    del ready_ref
    steps = sems.shape[0] - 2
    block, hidden = raw.shape[0] // steps, pair_ref.shape[2]

    def fetch(i):
        rows = pl.ds(i * block, block)
        return pltpu.make_async_copy(pair_ref.at[rows], raw.at[rows], sems.at[i])

    downs = [
        pltpu.make_async_copy(down_ref, down_out, sems.at[steps]),
        pltpu.make_async_copy(shared_ref, shared_out, sems.at[steps + 1]),
    ]
    for i in range(steps):
        fetch(i).start()
    for copy in downs:
        copy.start()
    for i in range(steps):
        fetch(i).wait()
        at = slice(i * block, (i + 1) * block)
        both = jnp.swapaxes(raw[at], 0, 1)
        flat_ref[at, :hidden] = both[0]
        flat_ref[at, hidden:] = both[1]
    for copy in downs:
        copy.wait()


def held_weights(pairs, down, shared, ready):
    depth, _, hidden = pairs.shape
    steps = 4
    operands = [pltpu.with_memory_space_constraint(x, pltpu.HBM) for x in (pairs, down, shared)]
    return pl.pallas_call(
        weights_kernel,
        in_specs=[pl.BlockSpec(memory_space=pltpu.HBM)] * 3 + [pl.BlockSpec(memory_space=pl.ANY)],
        out_specs=[pl.BlockSpec(memory_space=pltpu.VMEM)] * 3,
        out_shape=(
            jax.ShapeDtypeStruct((depth, 2 * hidden), pairs.dtype),
            jax.ShapeDtypeStruct(down.shape, down.dtype),
            jax.ShapeDtypeStruct(shared.shape, shared.dtype),
        ),
        scratch_shapes=[pltpu.VMEM(pairs.shape, pairs.dtype), pltpu.SemaphoreType.DMA((steps + 2,))],
        compiler_params=pltpu.CompilerParams(vmem_limit_bytes=VMEM_LIMIT),
        cost_estimate=pl.CostEstimate(
            flops=0, bytes_accessed=8 * depth * hidden, transcendentals=0
        ),
    )(*operands, ready)


def shared_up_kernel(rows_ref, up_ref, ready_ref, middle_ref, up, sums, sems):
    del ready_ref
    steps = sems.shape[0]
    block = up.shape[0] // steps

    def fetch(i):
        at = pl.ds(i * block, block)
        return pltpu.make_async_copy(up_ref.at[at], up.at[at], sems.at[i])

    for i in range(steps):
        fetch(i).start()
    for i in range(steps):
        fetch(i).wait()
        both = jnp.swapaxes(up[i * block:(i + 1) * block], 0, 1)
        left = rows_ref[:, i * block:(i + 1) * block]
        for half in range(2):
            term = jnp.dot(left, both[half], preferred_element_type=jnp.float32)
            sums[half] = term if i == 0 else sums[half] + term
    gate, lift = sums[0], sums[1]
    middle_ref[...] = (gate / (1.0 + jnp.exp(-gate)) * lift).astype(jnp.bfloat16)


def shared_middle(rows, up, ready):
    count, (width, _, hidden) = rows.shape[0], up.shape
    steps = 7
    return pl.pallas_call(
        shared_up_kernel,
        in_specs=[
            pl.BlockSpec(memory_space=pltpu.VMEM),
            pl.BlockSpec(memory_space=pltpu.HBM),
            pl.BlockSpec(memory_space=pl.ANY),
        ],
        out_specs=pl.BlockSpec(memory_space=pltpu.VMEM),
        out_shape=jax.ShapeDtypeStruct((count, hidden), jnp.bfloat16),
        scratch_shapes=[
            pltpu.VMEM(up.shape, up.dtype),
            pltpu.VMEM((2, count, hidden), jnp.float32),
            pltpu.SemaphoreType.DMA((steps,)),
        ],
        compiler_params=pltpu.CompilerParams(vmem_limit_bytes=20 << 20),
        cost_estimate=pl.CostEstimate(
            flops=4 * count * hidden * width,
            bytes_accessed=4 * hidden * width,
            transcendentals=0,
        ),
    )(rows, pltpu.with_memory_space_constraint(up, pltpu.HBM), ready)


def routed_kernel(pieces, half_ref, other_ref, flat_ref, down_ref, named_ref, shared_ref, keep_ref, send_ref, sums):
    depth, hidden = flat_ref.shape[0], flat_ref.shape[1] // 2
    rows, width = keep_ref.shape
    steps = 7
    block, piece = depth // steps, width // steps
    for i in range(steps):
        at = slice(i * block, (i + 1) * block)
        left = jnp.concatenate([half_ref[:, at], other_ref[:, at]], axis=0)
        term = jnp.dot(left, flat_ref[at, :], preferred_element_type=jnp.float32)
        sums[...] = term if i == 0 else sums[...] + term
    weight = jnp.concatenate([half_ref[:, depth:], other_ref[:, depth:]], axis=0)
    named = weight.astype(jnp.float32) * named_ref[...]
    weight = jnp.sum(named, axis=1, keepdims=True)
    gate, lift = sums[:, :hidden], sums[:, hidden:]
    sums[:, :hidden] = gate / (1.0 + jnp.exp(-gate)) * lift * weight
    ordered = [sums[first:first + count, :hidden] for first, count in pieces]
    middle = jnp.concatenate(ordered, axis=0).astype(jnp.bfloat16)
    own = shared_ref.shape[0] // CORES
    for i in range(steps):
        at = slice(i * piece, (i + 1) * piece)
        term = jnp.dot(middle, down_ref[:, at], preferred_element_type=jnp.float32)
        for core, out in enumerate((keep_ref, send_ref)):
            first = core * rows
            near = term[first:first + own] + shared_ref[core * own:(core + 1) * own, at]
            out[:, at] = jnp.concatenate([near, term[first + own:first + rows]], axis=0).astype(jnp.bfloat16)


def routed_parts(half, other, flat, down, named, shared, pieces):
    rows, width = half.shape[0], down.shape[1]
    return pl.pallas_call(
        functools.partial(routed_kernel, pieces),
        in_specs=[pl.BlockSpec(memory_space=pltpu.VMEM)] * 6,
        out_specs=[pl.BlockSpec(memory_space=pltpu.VMEM)] * CORES,
        out_shape=[jax.ShapeDtypeStruct((rows, width), jnp.bfloat16)] * CORES,
        scratch_shapes=[pltpu.VMEM((CORES * rows, flat.shape[1]), jnp.float32)],
        compiler_params=pltpu.CompilerParams(vmem_limit_bytes=VMEM_LIMIT),
        cost_estimate=pl.CostEstimate(
            flops=2 * CORES * rows * (flat.size + down.size),
            bytes_accessed=2 * (flat.size + down.size),
            transcendentals=0,
        ),
    )(half, other, flat, down, named, shared)


def after(value, ready):
    return lax.optimization_barrier((value, ready))[0]


def exchange(rows, axis, flip):
    size = lax.axis_size(axis)
    return lax.ppermute(rows, axis, [(i, i ^ flip) for i in range(size)])


def half_ep(rows, experts):
    parts = [exchange(rows, "ep", chip) for chip in range(CORES, experts, CORES)]
    return jnp.concatenate([rows] + parts, axis=0)


def chip_sum(pair, experts):
    count = pair.shape[0] * CORES // experts
    total = pair[:count].astype(jnp.float32)
    for chip in range(CORES, experts, CORES):
        at = chip // CORES * count
        total = total + exchange(pair[at:at + count], "ep", chip).astype(jnp.float32)
    return total


def per_device(tokens, routes, gates, expert_up, expert_down, shared_up, shared_down):
    count, width = tokens.shape
    experts = lax.axis_size("ep")
    subs = lax.axis_size("sub")
    me = lax.axis_index("ep")
    bf = jnp.bfloat16

    lanes = -(-experts // LANES) * LANES
    named = (lax.broadcasted_iota(jnp.int32, (1, lanes), 1) == me).astype(jnp.float32)
    routed_rows = owner_rows(tokens, routes, gates, named, lanes)
    token_half = half_ep(after(tokens, routed_rows), experts)

    order = list(range(2, subs))
    far = jnp.concatenate([exchange(routed_rows, "sub", k) for k in order], axis=0)
    own_half = half_ep(routed_rows, experts)
    near_half = exchange(own_half, "sub", 1)
    token_all = jnp.concatenate([token_half, exchange(token_half, "ep", 1)], axis=0)
    expert_weights, down_weights, shared_weights = held_weights(
        expert_up[0], expert_down[0], shared_down, routed_rows
    )
    far, expert_weights = lax.optimization_barrier((far, expert_weights))
    middle = shared_middle(token_all, shared_up, far)

    far_half = half_ep(far, experts)
    half = after(jnp.concatenate([own_half, near_half, far_half], axis=0), middle)
    other = exchange(half, "ep", 1)

    chips, split = experts // CORES, own_half.shape[0]
    pieces = []
    for core in range(CORES):
        first = core * half.shape[0]
        pieces.append((first, 2 * split))
        pieces += [
            (first + 2 * split + (chip * len(order) + at) * count, count)
            for at in range(len(order)) for chip in range(chips)
        ]
    shared_part = jnp.dot(middle, shared_weights, preferred_element_type=jnp.float32)
    keep, send = routed_parts(half, other, expert_weights, down_weights, named, shared_part, pieces)
    pair = (keep.astype(jnp.float32) + exchange(send, "ep", 1).astype(jnp.float32)).astype(bf)

    sums = [
        chip_sum(pair[at:at + split], experts).astype(bf)
        for at in range(2 * split, pair.shape[0], split)
    ]
    near = exchange(pair[split:2 * split], "sub", 1)
    near = (pair[:split].astype(jnp.float32) + near.astype(jnp.float32)).astype(bf)
    total = chip_sum(near, experts)
    for rows, k in zip(sums, order):
        total = total + exchange(rows, "sub", k).astype(jnp.float32)
    return total.astype(bf)


def solution(mesh):
    return jax.shard_map(
        per_device,
        mesh=mesh,
        in_specs=(
            P(("groups", "ep", "sub"), None),
            P(("groups", "ep", "sub"), None),
            P(("groups", "ep", "sub"), None),
            P("ep", None, None, "sub"),
            P("ep", "sub", None),
            P(None, None, "ep"),
            P("ep", None),
        ),
        out_specs=P(("groups", "ep", "sub"), None),
        check_vma=False,
    )
```

```python
import functools

import jax
import jax.numpy as jnp
from jax import lax
from jax.experimental import pallas as pl
from jax.experimental.pallas import tpu as pltpu
from jax.sharding import PartitionSpec as P

QBLOCK = 128
LANES = 128
CORES = 2
VMEM_LIMIT = 30 << 20


def owner_kernel(tokens_ref, routes_ref, gates_ref, ready_ref, routed_ref, tokens, routes, gates, sems):
    del ready_ref
    copies = [
        pltpu.make_async_copy(source, target, sems.at[i])
        for i, (source, target) in enumerate(
            ((tokens_ref, tokens), (routes_ref, routes), (gates_ref, gates))
        )
    ]
    for copy in copies:
        copy.start()
    for copy in copies:
        copy.wait()
    count, width = tokens.shape
    for at in range(0, width, QBLOCK):
        block = tokens[:, at:at + QBLOCK].astype(jnp.float32)
        largest = jnp.max(jnp.abs(block), axis=1, keepdims=True)
        scale = ((largest + 1e-06) / 448.0).astype(jnp.bfloat16).astype(jnp.float32)
        scaled = (block / scale).astype(jnp.bfloat16).astype(jnp.float32)
        routed_ref[:, at:at + QBLOCK] = (scaled * scale).astype(jnp.bfloat16)
    lanes = routed_ref.shape[1] - width
    expert = lax.broadcasted_iota(jnp.int32, (count, lanes), 1)
    diagonal = (
        lax.broadcasted_iota(jnp.int32, (count, count), 0)
        == lax.broadcasted_iota(jnp.int32, (count, count), 1)
    )

    def column(row):
        return jnp.sum(jnp.where(diagonal, row, 0), axis=1, keepdims=True)

    weight = jnp.zeros((count, lanes), jnp.float32)
    for k in range(routes.shape[0]):
        gate = column(gates[k:k + 1, :].astype(jnp.float32))
        named = column(routes[k:k + 1, :])
        weight = weight + jnp.where(named == expert, gate, 0.0)
    routed_ref[:, width:] = weight.astype(jnp.bfloat16)


def owner_rows(tokens, routes, gates, ready, lanes):
    count, width = tokens.shape
    operands = (tokens, routes.T, gates.T)
    return pl.pallas_call(
        owner_kernel,
        in_specs=[pl.BlockSpec(memory_space=pltpu.HBM)] * 3 + [pl.BlockSpec(memory_space=pl.ANY)],
        out_specs=pl.BlockSpec(memory_space=pltpu.VMEM),
        out_shape=jax.ShapeDtypeStruct((count, width + lanes), tokens.dtype),
        scratch_shapes=[pltpu.VMEM(x.shape, x.dtype) for x in operands]
        + [pltpu.SemaphoreType.DMA((len(operands),))],
        compiler_params=pltpu.CompilerParams(vmem_limit_bytes=4 << 20),
    )(*(pltpu.with_memory_space_constraint(x, pltpu.HBM) for x in operands), ready)


def weights_kernel(pair_ref, down_ref, shared_ref, ready_ref, flat_ref, down_out, shared_out, raw, sems):
    del ready_ref
    steps = sems.shape[0] - 2
    block, hidden = raw.shape[0] // steps, pair_ref.shape[2]

    def fetch(i):
        rows = pl.ds(i * block, block)
        return pltpu.make_async_copy(pair_ref.at[rows], raw.at[rows], sems.at[i])

    downs = [
        pltpu.make_async_copy(down_ref, down_out, sems.at[steps]),
        pltpu.make_async_copy(shared_ref, shared_out, sems.at[steps + 1]),
    ]
    for i in range(steps):
        fetch(i).start()
    for copy in downs:
        copy.start()
    for i in range(steps):
        fetch(i).wait()
        at = slice(i * block, (i + 1) * block)
        both = jnp.swapaxes(raw[at], 0, 1)
        flat_ref[at, :hidden] = both[0]
        flat_ref[at, hidden:] = both[1]
    for copy in downs:
        copy.wait()


def held_weights(pairs, down, shared, ready):
    depth, _, hidden = pairs.shape
    steps = 4
    operands = [pltpu.with_memory_space_constraint(x, pltpu.HBM) for x in (pairs, down, shared)]
    return pl.pallas_call(
        weights_kernel,
        in_specs=[pl.BlockSpec(memory_space=pltpu.HBM)] * 3 + [pl.BlockSpec(memory_space=pl.ANY)],
        out_specs=[pl.BlockSpec(memory_space=pltpu.VMEM)] * 3,
        out_shape=(
            jax.ShapeDtypeStruct((depth, 2 * hidden), pairs.dtype),
            jax.ShapeDtypeStruct(down.shape, down.dtype),
            jax.ShapeDtypeStruct(shared.shape, shared.dtype),
        ),
        scratch_shapes=[pltpu.VMEM(pairs.shape, pairs.dtype), pltpu.SemaphoreType.DMA((steps + 2,))],
        compiler_params=pltpu.CompilerParams(vmem_limit_bytes=VMEM_LIMIT),
        cost_estimate=pl.CostEstimate(
            flops=0, bytes_accessed=8 * depth * hidden, transcendentals=0
        ),
    )(*operands, ready)


def shared_up_kernel(rows_ref, up_ref, ready_ref, middle_ref, up, sums, sems):
    del ready_ref
    steps = sems.shape[0]
    block = up.shape[0] // steps

    def fetch(i):
        at = pl.ds(i * block, block)
        return pltpu.make_async_copy(up_ref.at[at], up.at[at], sems.at[i])

    for i in range(steps):
        fetch(i).start()
    for i in range(steps):
        fetch(i).wait()
        both = jnp.swapaxes(up[i * block:(i + 1) * block], 0, 1)
        left = rows_ref[:, i * block:(i + 1) * block]
        for half in range(2):
            term = jnp.dot(left, both[half], preferred_element_type=jnp.float32)
            sums[half] = term if i == 0 else sums[half] + term
    gate, lift = sums[0], sums[1]
    middle_ref[...] = (gate / (1.0 + jnp.exp(-gate)) * lift).astype(jnp.bfloat16)


def shared_middle(rows, up, ready):
    count, (width, _, hidden) = rows.shape[0], up.shape
    steps = 14
    return pl.pallas_call(
        shared_up_kernel,
        in_specs=[
            pl.BlockSpec(memory_space=pltpu.VMEM),
            pl.BlockSpec(memory_space=pltpu.HBM),
            pl.BlockSpec(memory_space=pl.ANY),
        ],
        out_specs=pl.BlockSpec(memory_space=pltpu.VMEM),
        out_shape=jax.ShapeDtypeStruct((count, hidden), jnp.bfloat16),
        scratch_shapes=[
            pltpu.VMEM(up.shape, up.dtype),
            pltpu.VMEM((2, count, hidden), jnp.float32),
            pltpu.SemaphoreType.DMA((steps,)),
        ],
        compiler_params=pltpu.CompilerParams(vmem_limit_bytes=20 << 20),
        cost_estimate=pl.CostEstimate(
            flops=4 * count * hidden * width,
            bytes_accessed=4 * hidden * width,
            transcendentals=0,
        ),
    )(rows, pltpu.with_memory_space_constraint(up, pltpu.HBM), ready)


def routed_kernel(pieces, half_ref, other_ref, flat_ref, down_ref, named_ref, shared_ref, keep_ref, send_ref, sums):
    depth, hidden = flat_ref.shape[0], flat_ref.shape[1] // 2
    rows, width = keep_ref.shape
    steps = 14
    block, piece = depth // steps, width // steps
    for i in range(steps):
        at = slice(i * block, (i + 1) * block)
        left = jnp.concatenate([half_ref[:, at], other_ref[:, at]], axis=0)
        term = jnp.dot(left, flat_ref[at, :], preferred_element_type=jnp.float32)
        sums[...] = term if i == 0 else sums[...] + term
    weight = jnp.concatenate([half_ref[:, depth:], other_ref[:, depth:]], axis=0)
    named = weight.astype(jnp.float32) * named_ref[...]
    weight = jnp.sum(named, axis=1, keepdims=True)
    gate, lift = sums[:, :hidden], sums[:, hidden:]
    sums[:, :hidden] = gate / (1.0 + jnp.exp(-gate)) * lift * weight
    ordered = [sums[first:first + count, :hidden] for first, count in pieces]
    middle = jnp.concatenate(ordered, axis=0).astype(jnp.bfloat16)
    own = shared_ref.shape[0] // CORES
    for i in range(steps):
        at = slice(i * piece, (i + 1) * piece)
        term = jnp.dot(middle, down_ref[:, at], preferred_element_type=jnp.float32)
        for core, out in enumerate((keep_ref, send_ref)):
            first = core * rows
            near = term[first:first + own] + shared_ref[core * own:(core + 1) * own, at]
            out[:, at] = jnp.concatenate([near, term[first + own:first + rows]], axis=0).astype(jnp.bfloat16)


def routed_parts(half, other, flat, down, named, shared, pieces):
    rows, width = half.shape[0], down.shape[1]
    return pl.pallas_call(
        functools.partial(routed_kernel, pieces),
        in_specs=[pl.BlockSpec(memory_space=pltpu.VMEM)] * 6,
        out_specs=[pl.BlockSpec(memory_space=pltpu.VMEM)] * CORES,
        out_shape=[jax.ShapeDtypeStruct((rows, width), jnp.bfloat16)] * CORES,
        scratch_shapes=[pltpu.VMEM((CORES * rows, flat.shape[1]), jnp.float32)],
        compiler_params=pltpu.CompilerParams(vmem_limit_bytes=VMEM_LIMIT),
        cost_estimate=pl.CostEstimate(
            flops=2 * CORES * rows * (flat.size + down.size),
            bytes_accessed=2 * (flat.size + down.size),
            transcendentals=0,
        ),
    )(half, other, flat, down, named, shared)


def after(value, ready):
    return lax.optimization_barrier((value, ready))[0]


def exchange(rows, axis, flip):
    size = lax.axis_size(axis)
    return lax.ppermute(rows, axis, [(i, i ^ flip) for i in range(size)])


def half_ep(rows, experts):
    parts = [exchange(rows, "ep", chip) for chip in range(CORES, experts, CORES)]
    return jnp.concatenate([rows] + parts, axis=0)


def chip_sum(pair, experts, earlier=None):
    count = pair.shape[0] * CORES // experts
    total = pair[:count].astype(jnp.float32)
    for chip in range(CORES, experts, CORES):
        at = chip // CORES * count
        other = exchange(pair[at:at + count], "ep", chip)
        if earlier is not None:
            other = after(other, earlier)
        total = total + other.astype(jnp.float32)
    return total


def per_device(tokens, routes, gates, expert_up, expert_down, shared_up, shared_down):
    count, width = tokens.shape
    experts = lax.axis_size("ep")
    subs = lax.axis_size("sub")
    me = lax.axis_index("ep")
    bf = jnp.bfloat16

    lanes = -(-experts // LANES) * LANES
    named = (lax.broadcasted_iota(jnp.int32, (1, lanes), 1) == me).astype(jnp.float32)
    routed_rows = owner_rows(tokens, routes, gates, named, lanes)
    token_half = half_ep(after(tokens, routed_rows), experts)

    order = list(range(subs - 1, 1, -1))
    far = jnp.concatenate([exchange(routed_rows, "sub", k) for k in order], axis=0)
    own_half = half_ep(routed_rows, experts)
    near_half = exchange(own_half, "sub", 1)
    token_all = jnp.concatenate([token_half, exchange(token_half, "ep", 1)], axis=0)
    expert_weights, down_weights, shared_weights = held_weights(
        expert_up[0], expert_down[0], shared_down, routed_rows
    )
    far, expert_weights = lax.optimization_barrier((far, expert_weights))
    middle = shared_middle(token_all, shared_up, far)

    far_half = half_ep(far, experts)
    half = after(jnp.concatenate([own_half, near_half, far_half], axis=0), middle)
    other = exchange(half, "ep", 1)

    chips, split = experts // CORES, own_half.shape[0]
    pieces = []
    for core in range(CORES):
        first = core * half.shape[0]
        pieces.append((first, 2 * split))
        pieces += [
            (first + 2 * split + (chip * len(order) + at) * count, count)
            for at in reversed(range(len(order))) for chip in range(chips)
        ]
    shared_part = jnp.dot(middle, shared_weights, preferred_element_type=jnp.float32)
    keep, send = routed_parts(half, other, expert_weights, down_weights, named, shared_part, pieces)
    pair = (keep.astype(jnp.float32) + exchange(send, "ep", 1).astype(jnp.float32)).astype(bf)

    sums = []
    for at in range(2 * split, pair.shape[0], split):
        earlier = sums[-1] if sums else None
        sums.append(chip_sum(pair[at:at + split], experts, earlier).astype(bf))
    near = exchange(pair[split:2 * split], "sub", 1)
    near = (pair[:split].astype(jnp.float32) + near.astype(jnp.float32)).astype(bf)
    total = chip_sum(near, experts)
    for rows, k in zip(sums, order[::-1]):
        total = total + exchange(rows, "sub", k).astype(jnp.float32)
    return total.astype(bf)


def solution(mesh):
    return jax.shard_map(
        per_device,
        mesh=mesh,
        in_specs=(
            P(("groups", "ep", "sub"), None),
            P(("groups", "ep", "sub"), None),
            P(("groups", "ep", "sub"), None),
            P("ep", None, None, "sub"),
            P("ep", "sub", None),
            P(None, None, "ep"),
            P("ep", None),
        ),
        out_specs=P(("groups", "ep", "sub"), None),
        check_vma=False,
    )
```

```python
import functools

import jax
import jax.numpy as jnp
from jax import lax
from jax.experimental import pallas as pl
from jax.experimental.pallas import tpu as pltpu
from jax.sharding import PartitionSpec as P

QBLOCK = 128
LANES = 128
CORES = 2
VMEM_LIMIT = 30 << 20
UP_BLOCKS = 14
EARLY_BLOCKS = 5
SPLIT_ROWS = 64


def owner_kernel(tokens_ref, routes_ref, gates_ref, ready_ref, routed_ref, tokens, routes, gates, sems):
    del ready_ref
    copies = [
        pltpu.make_async_copy(source, target, sems.at[i])
        for i, (source, target) in enumerate(
            ((tokens_ref, tokens), (routes_ref, routes), (gates_ref, gates))
        )
    ]
    for copy in copies:
        copy.start()
    for copy in copies:
        copy.wait()
    count, width = tokens.shape
    for at in range(0, width, QBLOCK):
        block = tokens[:, at:at + QBLOCK].astype(jnp.float32)
        largest = jnp.max(jnp.abs(block), axis=1, keepdims=True)
        scale = ((largest + 1e-06) / 448.0).astype(jnp.bfloat16).astype(jnp.float32)
        scaled = (block / scale).astype(jnp.bfloat16).astype(jnp.float32)
        routed_ref[:, at:at + QBLOCK] = (scaled * scale).astype(jnp.bfloat16)
    lanes = routed_ref.shape[1] - width
    expert = lax.broadcasted_iota(jnp.int32, (count, lanes), 1)
    diagonal = (
        lax.broadcasted_iota(jnp.int32, (count, count), 0)
        == lax.broadcasted_iota(jnp.int32, (count, count), 1)
    )

    def column(row):
        return jnp.sum(jnp.where(diagonal, row, 0), axis=1, keepdims=True)

    weight = jnp.zeros((count, lanes), jnp.float32)
    for k in range(routes.shape[0]):
        gate = column(gates[k:k + 1, :].astype(jnp.float32))
        named = column(routes[k:k + 1, :])
        weight = weight + jnp.where(named == expert, gate, 0.0)
    routed_ref[:, width:] = weight.astype(jnp.bfloat16)


def owner_rows(tokens, routes, gates, ready, lanes):
    count, width = tokens.shape
    operands = (tokens, routes.T, gates.T)
    return pl.pallas_call(
        owner_kernel,
        in_specs=[pl.BlockSpec(memory_space=pltpu.HBM)] * 3 + [pl.BlockSpec(memory_space=pl.ANY)],
        out_specs=pl.BlockSpec(memory_space=pltpu.VMEM),
        out_shape=jax.ShapeDtypeStruct((count, width + lanes), tokens.dtype),
        scratch_shapes=[pltpu.VMEM(x.shape, x.dtype) for x in operands]
        + [pltpu.SemaphoreType.DMA((len(operands),))],
        compiler_params=pltpu.CompilerParams(vmem_limit_bytes=4 << 20),
    )(*(pltpu.with_memory_space_constraint(x, pltpu.HBM) for x in operands), ready)


def split_kernel(pair_ref, up_ref, ready_ref, flat_ref, early_ref, raw, sems):
    del ready_ref
    steps = sems.shape[0] - 1
    block, hidden = raw.shape[0] // steps, pair_ref.shape[2]

    def fetch(i):
        rows = pl.ds(i * block, block)
        return pltpu.make_async_copy(pair_ref.at[rows], raw.at[rows], sems.at[i])

    early = pltpu.make_async_copy(up_ref.at[pl.ds(0, early_ref.shape[0])], early_ref, sems.at[steps])
    for i in range(steps):
        fetch(i).start()
    early.start()
    for i in range(steps):
        fetch(i).wait()
        for first in range(i * block, (i + 1) * block, SPLIT_ROWS):
            at = slice(first, first + SPLIT_ROWS)
            both = jnp.swapaxes(raw[at], 0, 1)
            flat_ref[at, :hidden] = both[0]
            flat_ref[at, hidden:] = both[1]
    early.wait()


def flat_pairs(pairs, up, ready):
    depth, _, hidden = pairs.shape
    steps = 7
    early = depth // UP_BLOCKS * EARLY_BLOCKS
    return pl.pallas_call(
        split_kernel,
        in_specs=[pl.BlockSpec(memory_space=pltpu.HBM)] * 2 + [pl.BlockSpec(memory_space=pl.ANY)],
        out_specs=[pl.BlockSpec(memory_space=pltpu.VMEM)] * 2,
        out_shape=(
            jax.ShapeDtypeStruct((depth, 2 * hidden), pairs.dtype),
            jax.ShapeDtypeStruct((early, *up.shape[1:]), up.dtype),
        ),
        scratch_shapes=[pltpu.VMEM(pairs.shape, pairs.dtype), pltpu.SemaphoreType.DMA((steps + 1,))],
        compiler_params=pltpu.CompilerParams(vmem_limit_bytes=VMEM_LIMIT),
        cost_estimate=pl.CostEstimate(
            flops=0, bytes_accessed=8 * depth * hidden, transcendentals=0
        ),
    )(*(pltpu.with_memory_space_constraint(x, pltpu.HBM) for x in (pairs, up)), ready)


def shared_up_kernel(rows_ref, early_ref, up_ref, ready_ref, middle_ref, up, sums, sems):
    del ready_ref
    late, early = sems.shape[0], early_ref.shape[0]
    block = up.shape[0] // late

    def fetch(i):
        at = pl.ds(i * block, block)
        return pltpu.make_async_copy(up_ref.at[pl.ds(early + i * block, block)], up.at[at], sems.at[i])

    for i in range(late):
        fetch(i).start()
    for i in range(early // block + late):
        at = i * block - early
        if at >= 0:
            fetch(at // block).wait()
            pairs = up[at:at + block]
        else:
            pairs = early_ref[i * block:(i + 1) * block]
        both = jnp.swapaxes(pairs, 0, 1)
        left = rows_ref[:, i * block:(i + 1) * block]
        for half in range(2):
            term = jnp.dot(left, both[half], preferred_element_type=jnp.float32)
            sums[half] = term if i == 0 else sums[half] + term
    gate, lift = sums[0], sums[1]
    middle_ref[...] = (gate / (1.0 + jnp.exp(-gate)) * lift).astype(jnp.bfloat16)


def shared_middle(rows, early, up, ready):
    count, (width, _, hidden) = rows.shape[0], up.shape
    late = width - early.shape[0]
    return pl.pallas_call(
        shared_up_kernel,
        in_specs=[
            pl.BlockSpec(memory_space=pltpu.VMEM),
            pl.BlockSpec(memory_space=pltpu.VMEM),
            pl.BlockSpec(memory_space=pltpu.HBM),
            pl.BlockSpec(memory_space=pl.ANY),
        ],
        out_specs=pl.BlockSpec(memory_space=pltpu.VMEM),
        out_shape=jax.ShapeDtypeStruct((count, hidden), jnp.bfloat16),
        scratch_shapes=[
            pltpu.VMEM((late, *up.shape[1:]), up.dtype),
            pltpu.VMEM((2, count, hidden), jnp.float32),
            pltpu.SemaphoreType.DMA((UP_BLOCKS - EARLY_BLOCKS,)),
        ],
        compiler_params=pltpu.CompilerParams(vmem_limit_bytes=20 << 20),
        cost_estimate=pl.CostEstimate(
            flops=4 * count * hidden * width,
            bytes_accessed=4 * hidden * width,
            transcendentals=0,
        ),
    )(rows, early, pltpu.with_memory_space_constraint(up, pltpu.HBM), ready)


def routed_kernel(pieces, *refs):
    rows_refs = refs[:2 * CORES]
    flat_ref, down_ref, named_ref, shared_ref, keep_ref, near_ref, far_ref, sums = refs[2 * CORES:]
    depth, hidden = flat_ref.shape[0], flat_ref.shape[1] // 2
    rows, width = keep_ref.shape
    steps = 14
    block, piece = depth // steps, width // steps
    for i in range(steps):
        at = slice(i * block, (i + 1) * block)
        left = jnp.concatenate([ref[:, at] for ref in rows_refs], axis=0)
        term = jnp.dot(left, flat_ref[at, :], preferred_element_type=jnp.float32)
        sums[...] = term if i == 0 else sums[...] + term
    weight = jnp.concatenate([ref[:, depth:] for ref in rows_refs], axis=0)
    named = weight.astype(jnp.float32) * named_ref[...]
    weight = jnp.sum(named, axis=1, keepdims=True)
    gate, lift = sums[:, :hidden], sums[:, hidden:]
    sums[:, :hidden] = gate / (1.0 + jnp.exp(-gate)) * lift * weight
    ordered = [sums[first:first + count, :hidden] for first, count in pieces]
    middle = jnp.concatenate(ordered, axis=0).astype(jnp.bfloat16)
    own, near = shared_ref.shape[0] // CORES, near_ref.shape[0]
    for i in range(steps):
        at = slice(i * piece, (i + 1) * piece)
        term = jnp.dot(middle, down_ref[:, at], preferred_element_type=jnp.float32)
        shared = shared_ref[:, at]
        first = jnp.concatenate([term[:own] + shared[:own], term[own:rows]], axis=0)
        keep_ref[:, at] = first.astype(jnp.bfloat16)
        second = [term[rows:rows + own] + shared[own:], term[rows + own:rows + near]]
        near_ref[:, at] = jnp.concatenate(second, axis=0).astype(jnp.bfloat16)
        far_ref[:, at] = term[rows + near:].astype(jnp.bfloat16)


def routed_parts(gathered, flat, down, named, shared, pieces, near):
    count, width = sum(rows.shape[0] for rows in gathered), down.shape[1]
    half = count // CORES
    return pl.pallas_call(
        functools.partial(routed_kernel, pieces),
        in_specs=[pl.BlockSpec(memory_space=pltpu.VMEM)] * (len(gathered) + 4),
        out_specs=[pl.BlockSpec(memory_space=pltpu.VMEM)] * 3,
        out_shape=[jax.ShapeDtypeStruct((rows, width), jnp.bfloat16) for rows in (half, near, half - near)],
        scratch_shapes=[pltpu.VMEM((count, flat.shape[1]), jnp.float32)],
        compiler_params=pltpu.CompilerParams(vmem_limit_bytes=VMEM_LIMIT),
        cost_estimate=pl.CostEstimate(
            flops=2 * count * (flat.size + down.size),
            bytes_accessed=2 * (flat.size + down.size),
            transcendentals=0,
        ),
    )(*gathered, flat, down, named, shared)


def after(value, ready):
    return lax.optimization_barrier((value, ready))[0]


def exchange(rows, axis, flip):
    size = lax.axis_size(axis)
    return lax.ppermute(rows, axis, [(i, i ^ flip) for i in range(size)])


def half_ep(rows, experts):
    parts = [exchange(rows, "ep", chip) for chip in range(CORES, experts, CORES)]
    return jnp.concatenate([rows] + parts, axis=0)


def chip_sum(pair, experts, earlier=None):
    count = pair.shape[0] * CORES // experts
    total = pair[:count].astype(jnp.float32)
    for chip in range(CORES, experts, CORES):
        at = chip // CORES * count
        other = exchange(pair[at:at + count], "ep", chip)
        if earlier is not None:
            other = after(other, earlier)
        total = total + other.astype(jnp.float32)
    return total


def per_device(tokens, routes, gates, expert_up, expert_down, shared_up, shared_down):
    count, width = tokens.shape
    experts = lax.axis_size("ep")
    subs = lax.axis_size("sub")
    me = lax.axis_index("ep")
    bf = jnp.bfloat16

    lanes = -(-experts // LANES) * LANES
    named = (lax.broadcasted_iota(jnp.int32, (1, lanes), 1) == me).astype(jnp.float32)
    routed_rows = owner_rows(tokens, routes, gates, named, lanes)
    token_half = half_ep(after(tokens, routed_rows), experts)

    order = list(range(subs - 1, 1, -1))
    far = jnp.concatenate([exchange(routed_rows, "sub", k) for k in order], axis=0)
    own_half = half_ep(routed_rows, experts)
    near_half = exchange(own_half, "sub", 1)
    token_all = jnp.concatenate([token_half, exchange(token_half, "ep", 1)], axis=0)
    expert_weights, early = flat_pairs(expert_up[0], shared_up, routed_rows)
    far, expert_weights = lax.optimization_barrier((far, expert_weights))
    middle = shared_middle(token_all, early, shared_up, far)

    far_chips = [exchange(far, "ep", chip) for chip in range(CORES, experts, CORES)]
    first = jnp.concatenate([own_half, far], axis=0)
    late = after(jnp.concatenate([near_half] + far_chips, axis=0), middle)
    gathered = (first, late, exchange(first, "ep", 1), exchange(late, "ep", 1))

    chips, split = experts // CORES, own_half.shape[0]
    pieces = []
    for core in range(CORES):
        at_first = core * (first.shape[0] + late.shape[0])
        at_late = at_first + first.shape[0]
        pieces += [(at_first, split), (at_late, split)]
        for at in reversed(range(len(order))):
            pieces.append((at_first + split + at * count, count))
            pieces += [
                (at_late + split + (chip * len(order) + at) * count, count) for chip in range(chips - 1)
            ]
    shared_part = jnp.dot(middle, shared_down, preferred_element_type=jnp.float32)
    keep, send_near, send_far = routed_parts(
        gathered, expert_weights, expert_down[0], named, shared_part, pieces, 2 * split
    )

    def pair_sum(own, send):
        return (own.astype(jnp.float32) + exchange(send, "ep", 1).astype(jnp.float32)).astype(bf)

    pair = pair_sum(keep[2 * split:], send_far)
    sums = []
    for at in range(0, pair.shape[0], split):
        earlier = sums[-1] if sums else None
        sums.append(chip_sum(pair[at:at + split], experts, earlier).astype(bf))
    pair = pair_sum(keep[:2 * split], send_near)
    near = exchange(pair[split:], "sub", 1)
    near = (pair[:split].astype(jnp.float32) + near.astype(jnp.float32)).astype(bf)
    total = chip_sum(near, experts)
    for rows, k in zip(sums, order[::-1]):
        total = total + exchange(rows, "sub", k).astype(jnp.float32)
    return total.astype(bf)


def solution(mesh):
    return jax.shard_map(
        per_device,
        mesh=mesh,
        in_specs=(
            P(("groups", "ep", "sub"), None),
            P(("groups", "ep", "sub"), None),
            P(("groups", "ep", "sub"), None),
            P("ep", None, None, "sub"),
            P("ep", "sub", None),
            P(None, None, "ep"),
            P("ep", None),
        ),
        out_specs=P(("groups", "ep", "sub"), None),
        check_vma=False,
    )
```

```python
import functools

import jax
import jax.numpy as jnp
from jax import lax
from jax.experimental import pallas as pl
from jax.experimental.pallas import tpu as pltpu
from jax.sharding import PartitionSpec as P

QBLOCK = 128
LANES = 128
CORES = 2
VMEM_LIMIT = 30 << 20
UP_BLOCKS = 14
EARLY_BLOCKS = 5
SPLIT_ROWS = 64


def owner_kernel(tokens_ref, routes_ref, gates_ref, ready_ref, routed_ref, tokens, routes, gates, sems):
    del ready_ref
    copies = [
        pltpu.make_async_copy(source, target, sems.at[i])
        for i, (source, target) in enumerate(
            ((tokens_ref, tokens), (routes_ref, routes), (gates_ref, gates))
        )
    ]
    for copy in copies:
        copy.start()
    for copy in copies:
        copy.wait()
    count, width = tokens.shape
    for at in range(0, width, QBLOCK):
        block = tokens[:, at:at + QBLOCK].astype(jnp.float32)
        largest = jnp.max(jnp.abs(block), axis=1, keepdims=True)
        scale = ((largest + 1e-06) / 448.0).astype(jnp.bfloat16).astype(jnp.float32)
        scaled = (block / scale).astype(jnp.bfloat16).astype(jnp.float32)
        routed_ref[:, at:at + QBLOCK] = (scaled * scale).astype(jnp.bfloat16)
    lanes = routed_ref.shape[1] - width
    expert = lax.broadcasted_iota(jnp.int32, (count, lanes), 1)
    diagonal = (
        lax.broadcasted_iota(jnp.int32, (count, count), 0)
        == lax.broadcasted_iota(jnp.int32, (count, count), 1)
    )

    def column(row):
        return jnp.sum(jnp.where(diagonal, row, 0), axis=1, keepdims=True)

    weight = jnp.zeros((count, lanes), jnp.float32)
    for k in range(routes.shape[0]):
        gate = column(gates[k:k + 1, :].astype(jnp.float32))
        named = column(routes[k:k + 1, :])
        weight = weight + jnp.where(named == expert, gate, 0.0)
    routed_ref[:, width:] = weight.astype(jnp.bfloat16)


def owner_rows(tokens, routes, gates, ready, lanes):
    count, width = tokens.shape
    operands = (tokens, routes.T, gates.T)
    return pl.pallas_call(
        owner_kernel,
        in_specs=[pl.BlockSpec(memory_space=pltpu.HBM)] * 3 + [pl.BlockSpec(memory_space=pl.ANY)],
        out_specs=pl.BlockSpec(memory_space=pltpu.VMEM),
        out_shape=jax.ShapeDtypeStruct((count, width + lanes), tokens.dtype),
        scratch_shapes=[pltpu.VMEM(x.shape, x.dtype) for x in operands]
        + [pltpu.SemaphoreType.DMA((len(operands),))],
        compiler_params=pltpu.CompilerParams(vmem_limit_bytes=4 << 20),
    )(*(pltpu.with_memory_space_constraint(x, pltpu.HBM) for x in operands), ready)


def split_kernel(pair_ref, up_ref, ready_ref, flat_ref, early_ref, raw, sems):
    del ready_ref
    steps = sems.shape[0] - 1
    block, hidden = raw.shape[0] // steps, pair_ref.shape[2]

    def fetch(i):
        rows = pl.ds(i * block, block)
        return pltpu.make_async_copy(pair_ref.at[rows], raw.at[rows], sems.at[i])

    early = pltpu.make_async_copy(up_ref.at[pl.ds(0, early_ref.shape[0])], early_ref, sems.at[steps])
    for i in range(steps):
        fetch(i).start()
    early.start()
    for i in range(steps):
        fetch(i).wait()
        for first in range(i * block, (i + 1) * block, SPLIT_ROWS):
            at = slice(first, first + SPLIT_ROWS)
            both = jnp.swapaxes(raw[at], 0, 1)
            flat_ref[at, :hidden] = both[0]
            flat_ref[at, hidden:] = both[1]
    early.wait()


def flat_pairs(pairs, up, ready):
    depth, _, hidden = pairs.shape
    steps = 7
    early = depth // UP_BLOCKS * EARLY_BLOCKS
    return pl.pallas_call(
        split_kernel,
        in_specs=[pl.BlockSpec(memory_space=pltpu.HBM)] * 2 + [pl.BlockSpec(memory_space=pl.ANY)],
        out_specs=[pl.BlockSpec(memory_space=pltpu.VMEM)] * 2,
        out_shape=(
            jax.ShapeDtypeStruct((depth, 2 * hidden), pairs.dtype),
            jax.ShapeDtypeStruct((early, *up.shape[1:]), up.dtype),
        ),
        scratch_shapes=[pltpu.VMEM(pairs.shape, pairs.dtype), pltpu.SemaphoreType.DMA((steps + 1,))],
        compiler_params=pltpu.CompilerParams(vmem_limit_bytes=VMEM_LIMIT),
        cost_estimate=pl.CostEstimate(
            flops=0, bytes_accessed=8 * depth * hidden, transcendentals=0
        ),
    )(*(pltpu.with_memory_space_constraint(x, pltpu.HBM) for x in (pairs, up)), ready)


def shared_up_kernel(rows_ref, early_ref, up_ref, ready_ref, middle_ref, up, sums, sems):
    del ready_ref
    late, early = sems.shape[0], early_ref.shape[0]
    block = up.shape[0] // late

    def fetch(i):
        at = pl.ds(i * block, block)
        return pltpu.make_async_copy(up_ref.at[pl.ds(early + i * block, block)], up.at[at], sems.at[i])

    for i in range(late):
        fetch(i).start()
    for i in range(early // block + late):
        at = i * block - early
        if at >= 0:
            fetch(at // block).wait()
            pairs = up[at:at + block]
        else:
            pairs = early_ref[i * block:(i + 1) * block]
        both = jnp.swapaxes(pairs, 0, 1)
        left = rows_ref[:, i * block:(i + 1) * block]
        for half in range(2):
            term = jnp.dot(left, both[half], preferred_element_type=jnp.float32)
            sums[half] = term if i == 0 else sums[half] + term
    gate, lift = sums[0], sums[1]
    middle_ref[...] = (gate / (1.0 + jnp.exp(-gate)) * lift).astype(jnp.bfloat16)


def shared_middle(rows, early, up, ready):
    count, (width, _, hidden) = rows.shape[0], up.shape
    late = width - early.shape[0]
    return pl.pallas_call(
        shared_up_kernel,
        in_specs=[
            pl.BlockSpec(memory_space=pltpu.VMEM),
            pl.BlockSpec(memory_space=pltpu.VMEM),
            pl.BlockSpec(memory_space=pltpu.HBM),
            pl.BlockSpec(memory_space=pl.ANY),
        ],
        out_specs=pl.BlockSpec(memory_space=pltpu.VMEM),
        out_shape=jax.ShapeDtypeStruct((count, hidden), jnp.bfloat16),
        scratch_shapes=[
            pltpu.VMEM((late, *up.shape[1:]), up.dtype),
            pltpu.VMEM((2, count, hidden), jnp.float32),
            pltpu.SemaphoreType.DMA((UP_BLOCKS - EARLY_BLOCKS,)),
        ],
        compiler_params=pltpu.CompilerParams(vmem_limit_bytes=20 << 20),
        cost_estimate=pl.CostEstimate(
            flops=4 * count * hidden * width,
            bytes_accessed=4 * hidden * width,
            transcendentals=0,
        ),
    )(rows, early, pltpu.with_memory_space_constraint(up, pltpu.HBM), ready)


def routed_kernel(pieces, *refs):
    rows_refs = refs[:2 * CORES]
    flat_ref, down_ref, named_ref, shared_ref, keep_ref, near_ref, far_ref, sums = refs[2 * CORES:]
    depth, hidden = flat_ref.shape[0], flat_ref.shape[1] // 2
    rows, width = keep_ref.shape
    steps = 14
    block, piece = depth // steps, width // steps
    for i in range(steps):
        at = slice(i * block, (i + 1) * block)
        left = jnp.concatenate([ref[:, at] for ref in rows_refs], axis=0)
        term = jnp.dot(left, flat_ref[at, :], preferred_element_type=jnp.float32)
        sums[...] = term if i == 0 else sums[...] + term
    weight = jnp.concatenate([ref[:, depth:] for ref in rows_refs], axis=0)
    named = weight.astype(jnp.float32) * named_ref[...]
    weight = jnp.sum(named, axis=1, keepdims=True)
    gate, lift = sums[:, :hidden], sums[:, hidden:]
    sums[:, :hidden] = gate / (1.0 + jnp.exp(-gate)) * lift * weight
    ordered = [sums[first:first + count, :hidden] for first, count in pieces]
    middle = jnp.concatenate(ordered, axis=0).astype(jnp.bfloat16)
    own, near = shared_ref.shape[0] // CORES, near_ref.shape[0]
    for i in range(steps):
        at = slice(i * piece, (i + 1) * piece)
        term = jnp.dot(middle, down_ref[:, at], preferred_element_type=jnp.float32)
        shared = shared_ref[:, at]
        first = jnp.concatenate([term[:own] + shared[:own], term[own:rows]], axis=0)
        keep_ref[:, at] = first.astype(jnp.bfloat16)
        second = [term[rows:rows + own] + shared[own:], term[rows + own:rows + near]]
        near_ref[:, at] = jnp.concatenate(second, axis=0).astype(jnp.bfloat16)
        far_ref[:, at] = term[rows + near:].astype(jnp.bfloat16)


def routed_parts(gathered, flat, down, named, shared, pieces, near):
    count, width = sum(rows.shape[0] for rows in gathered), down.shape[1]
    half = count // CORES
    return pl.pallas_call(
        functools.partial(routed_kernel, pieces),
        in_specs=[pl.BlockSpec(memory_space=pltpu.VMEM)] * (len(gathered) + 4),
        out_specs=[pl.BlockSpec(memory_space=pltpu.VMEM)] * 3,
        out_shape=[jax.ShapeDtypeStruct((rows, width), jnp.bfloat16) for rows in (half, near, half - near)],
        scratch_shapes=[pltpu.VMEM((count, flat.shape[1]), jnp.float32)],
        compiler_params=pltpu.CompilerParams(vmem_limit_bytes=VMEM_LIMIT),
        cost_estimate=pl.CostEstimate(
            flops=2 * count * (flat.size + down.size),
            bytes_accessed=2 * (flat.size + down.size),
            transcendentals=0,
        ),
    )(*gathered, flat, down, named, shared)


def after(value, ready):
    return lax.optimization_barrier((value, ready))[0]


def exchange(rows, axis, flip):
    size = lax.axis_size(axis)
    return lax.ppermute(rows, axis, [(i, i ^ flip) for i in range(size)])


def half_ep(rows, experts):
    parts = [exchange(rows, "ep", chip) for chip in range(CORES, experts, CORES)]
    return jnp.concatenate([rows] + parts, axis=0)


def chip_sum(pair, experts, earlier=None):
    count = pair.shape[0] * CORES // experts
    total = pair[:count].astype(jnp.float32)
    for chip in range(CORES, experts, CORES):
        at = chip // CORES * count
        other = exchange(pair[at:at + count], "ep", chip)
        if earlier is not None:
            other = after(other, earlier)
        total = total + other.astype(jnp.float32)
    return total


def per_device(tokens, routes, gates, expert_up, expert_down, shared_up, shared_down):
    count, width = tokens.shape
    experts = lax.axis_size("ep")
    subs = lax.axis_size("sub")
    me = lax.axis_index("ep")
    bf = jnp.bfloat16

    lanes = -(-experts // LANES) * LANES
    named = (lax.broadcasted_iota(jnp.int32, (1, lanes), 1) == me).astype(jnp.float32)
    routed_rows = owner_rows(tokens, routes, gates, named, lanes)
    token_half = half_ep(after(tokens, routed_rows), experts)

    order = list(range(subs - 1, 1, -1))
    far = jnp.concatenate([exchange(routed_rows, "sub", k) for k in order], axis=0)
    own_half = half_ep(routed_rows, experts)
    near_half = exchange(own_half, "sub", 1)
    token_all = jnp.concatenate([token_half, exchange(token_half, "ep", 1)], axis=0)
    expert_weights, early = flat_pairs(expert_up[0], shared_up, routed_rows)
    far, expert_weights, _ = lax.optimization_barrier((far, expert_weights, (own_half, token_half)))
    middle = shared_middle(token_all, early, shared_up, far)

    far_chips = [exchange(far, "ep", chip) for chip in range(CORES, experts, CORES)]
    first = jnp.concatenate([own_half, far], axis=0)
    late = after(jnp.concatenate([near_half] + far_chips, axis=0), middle)
    gathered = (first, late, exchange(first, "ep", 1), exchange(late, "ep", 1))

    chips, split = experts // CORES, own_half.shape[0]
    pieces = []
    for core in range(CORES):
        at_first = core * (first.shape[0] + late.shape[0])
        at_late = at_first + first.shape[0]
        pieces += [(at_first, split), (at_late, split)]
        for at in reversed(range(len(order))):
            pieces.append((at_first + split + at * count, count))
            pieces += [
                (at_late + split + (chip * len(order) + at) * count, count) for chip in range(chips - 1)
            ]
    shared_part = jnp.dot(middle, shared_down, preferred_element_type=jnp.float32)
    keep, send_near, send_far = routed_parts(
        gathered, expert_weights, expert_down[0], named, shared_part, pieces, 2 * split
    )

    def pair_sum(own, send):
        return (own.astype(jnp.float32) + exchange(send, "ep", 1).astype(jnp.float32)).astype(bf)

    pair = pair_sum(keep[2 * split:], send_far)
    sums = []
    for at in range(0, pair.shape[0], split):
        earlier = sums[-1] if sums else None
        sums.append(chip_sum(pair[at:at + split], experts, earlier).astype(bf))
    pair = pair_sum(keep[:2 * split], send_near)
    near = exchange(pair[split:], "sub", 1)
    near = (pair[:split].astype(jnp.float32) + near.astype(jnp.float32)).astype(bf)
    total = chip_sum(near, experts)
    for rows, k in zip(sums, order[::-1]):
        total = total + exchange(rows, "sub", k).astype(jnp.float32)
    return total.astype(bf)


def solution(mesh):
    return jax.shard_map(
        per_device,
        mesh=mesh,
        in_specs=(
            P(("groups", "ep", "sub"), None),
            P(("groups", "ep", "sub"), None),
            P(("groups", "ep", "sub"), None),
            P("ep", None, None, "sub"),
            P("ep", "sub", None),
            P(None, None, "ep"),
            P("ep", None),
        ),
        out_specs=P(("groups", "ep", "sub"), None),
        check_vma=False,
    )
```

```python
import functools

import jax
import jax.numpy as jnp
from jax import lax
from jax.experimental import pallas as pl
from jax.experimental.pallas import tpu as pltpu
from jax.sharding import PartitionSpec as P

QBLOCK = 128
LANES = 128
CORES = 2
VMEM_LIMIT = 30 << 20
UP_BLOCKS = 14
EARLY_BLOCKS = 5
SPLIT_ROWS = 64


def owner_kernel(tokens_ref, routes_ref, gates_ref, ready_ref, routed_ref, tokens, routes, gates, sems):
    del ready_ref
    copies = [
        pltpu.make_async_copy(source, target, sems.at[i])
        for i, (source, target) in enumerate(
            ((tokens_ref, tokens), (routes_ref, routes), (gates_ref, gates))
        )
    ]
    for copy in copies:
        copy.start()
    for copy in copies:
        copy.wait()
    count, width = tokens.shape
    for at in range(0, width, QBLOCK):
        block = tokens[:, at:at + QBLOCK].astype(jnp.float32)
        largest = jnp.max(jnp.abs(block), axis=1, keepdims=True)
        scale = ((largest + 1e-06) / 448.0).astype(jnp.bfloat16).astype(jnp.float32)
        scaled = (block / scale).astype(jnp.bfloat16).astype(jnp.float32)
        routed_ref[:, at:at + QBLOCK] = (scaled * scale).astype(jnp.bfloat16)
    lanes = routed_ref.shape[1] - width
    expert = lax.broadcasted_iota(jnp.int32, (count, lanes), 1)
    diagonal = (
        lax.broadcasted_iota(jnp.int32, (count, count), 0)
        == lax.broadcasted_iota(jnp.int32, (count, count), 1)
    )

    def column(row):
        return jnp.sum(jnp.where(diagonal, row, 0), axis=1, keepdims=True)

    weight = jnp.zeros((count, lanes), jnp.float32)
    for k in range(routes.shape[0]):
        gate = column(gates[k:k + 1, :].astype(jnp.float32))
        named = column(routes[k:k + 1, :])
        weight = weight + jnp.where(named == expert, gate, 0.0)
    routed_ref[:, width:] = weight.astype(jnp.bfloat16)


def owner_rows(tokens, routes, gates, ready, lanes):
    count, width = tokens.shape
    operands = (tokens, routes.T, gates.T)
    return pl.pallas_call(
        owner_kernel,
        in_specs=[pl.BlockSpec(memory_space=pltpu.HBM)] * 3 + [pl.BlockSpec(memory_space=pl.ANY)],
        out_specs=pl.BlockSpec(memory_space=pltpu.VMEM),
        out_shape=jax.ShapeDtypeStruct((count, width + lanes), tokens.dtype),
        scratch_shapes=[pltpu.VMEM(x.shape, x.dtype) for x in operands]
        + [pltpu.SemaphoreType.DMA((len(operands),))],
        compiler_params=pltpu.CompilerParams(vmem_limit_bytes=4 << 20),
    )(*(pltpu.with_memory_space_constraint(x, pltpu.HBM) for x in operands), ready)


def split_kernel(pair_ref, up_ref, ready_ref, flat_ref, early_ref, raw, sems):
    del ready_ref
    steps = sems.shape[0] - 1
    block, hidden = raw.shape[0] // steps, pair_ref.shape[2]

    def fetch(i):
        rows = pl.ds(i * block, block)
        return pltpu.make_async_copy(pair_ref.at[rows], raw.at[rows], sems.at[i])

    early = pltpu.make_async_copy(up_ref.at[pl.ds(0, early_ref.shape[0])], early_ref, sems.at[steps])
    for i in range(steps):
        fetch(i).start()
    early.start()
    for i in range(steps):
        fetch(i).wait()
        for first in range(i * block, (i + 1) * block, SPLIT_ROWS):
            at = slice(first, first + SPLIT_ROWS)
            both = jnp.swapaxes(raw[at], 0, 1)
            flat_ref[at, :hidden] = both[0]
            flat_ref[at, hidden:] = both[1]
    early.wait()


def flat_pairs(pairs, up, ready):
    depth, _, hidden = pairs.shape
    steps = 7
    early = depth // UP_BLOCKS * EARLY_BLOCKS
    return pl.pallas_call(
        split_kernel,
        in_specs=[pl.BlockSpec(memory_space=pltpu.HBM)] * 2 + [pl.BlockSpec(memory_space=pl.ANY)],
        out_specs=[pl.BlockSpec(memory_space=pltpu.VMEM)] * 2,
        out_shape=(
            jax.ShapeDtypeStruct((depth, 2 * hidden), pairs.dtype),
            jax.ShapeDtypeStruct((early, *up.shape[1:]), up.dtype),
        ),
        scratch_shapes=[pltpu.VMEM(pairs.shape, pairs.dtype), pltpu.SemaphoreType.DMA((steps + 1,))],
        compiler_params=pltpu.CompilerParams(vmem_limit_bytes=VMEM_LIMIT),
        cost_estimate=pl.CostEstimate(
            flops=0, bytes_accessed=8 * depth * hidden, transcendentals=0
        ),
    )(*(pltpu.with_memory_space_constraint(x, pltpu.HBM) for x in (pairs, up)), ready)


def shared_up_kernel(rows_ref, early_ref, up_ref, ready_ref, middle_ref, up, sums, sems):
    del ready_ref
    late, early = sems.shape[0], early_ref.shape[0]
    block = up.shape[0] // late

    def fetch(i):
        at = pl.ds(i * block, block)
        return pltpu.make_async_copy(up_ref.at[pl.ds(early + i * block, block)], up.at[at], sems.at[i])

    for i in range(late):
        fetch(i).start()
    for i in range(early // block + late):
        at = i * block - early
        if at >= 0:
            fetch(at // block).wait()
            pairs = up[at:at + block]
        else:
            pairs = early_ref[i * block:(i + 1) * block]
        both = jnp.swapaxes(pairs, 0, 1)
        left = rows_ref[:, i * block:(i + 1) * block]
        for half in range(2):
            term = jnp.dot(left, both[half], preferred_element_type=jnp.float32)
            sums[half] = term if i == 0 else sums[half] + term
    gate, lift = sums[0], sums[1]
    middle_ref[...] = (gate / (1.0 + jnp.exp(-gate)) * lift).astype(jnp.bfloat16)


def shared_middle(rows, early, up, ready):
    count, (width, _, hidden) = rows.shape[0], up.shape
    late = width - early.shape[0]
    return pl.pallas_call(
        shared_up_kernel,
        in_specs=[
            pl.BlockSpec(memory_space=pltpu.VMEM),
            pl.BlockSpec(memory_space=pltpu.VMEM),
            pl.BlockSpec(memory_space=pltpu.HBM),
            pl.BlockSpec(memory_space=pl.ANY),
        ],
        out_specs=pl.BlockSpec(memory_space=pltpu.VMEM),
        out_shape=jax.ShapeDtypeStruct((count, hidden), jnp.bfloat16),
        scratch_shapes=[
            pltpu.VMEM((late, *up.shape[1:]), up.dtype),
            pltpu.VMEM((2, count, hidden), jnp.float32),
            pltpu.SemaphoreType.DMA((UP_BLOCKS - EARLY_BLOCKS,)),
        ],
        compiler_params=pltpu.CompilerParams(vmem_limit_bytes=20 << 20),
        cost_estimate=pl.CostEstimate(
            flops=4 * count * hidden * width,
            bytes_accessed=4 * hidden * width,
            transcendentals=0,
        ),
    )(rows, early, pltpu.with_memory_space_constraint(up, pltpu.HBM), ready)


def routed_kernel(pieces, *refs):
    rows_refs = refs[:2 * CORES]
    flat_ref, down_ref, named_ref, shared_ref, keep_ref, near_ref, far_ref, sums = refs[2 * CORES:]
    depth, hidden = flat_ref.shape[0], flat_ref.shape[1] // 2
    rows, width = keep_ref.shape
    steps = 14
    block, piece = depth // steps, width // steps
    for i in range(steps):
        at = slice(i * block, (i + 1) * block)
        left = jnp.concatenate([ref[:, at] for ref in rows_refs], axis=0)
        term = jnp.dot(left, flat_ref[at, :], preferred_element_type=jnp.float32)
        sums[...] = term if i == 0 else sums[...] + term
    weight = jnp.concatenate([ref[:, depth:] for ref in rows_refs], axis=0)
    named = weight.astype(jnp.float32) * named_ref[...]
    weight = jnp.sum(named, axis=1, keepdims=True)
    gate, lift = sums[:, :hidden], sums[:, hidden:]
    sums[:, :hidden] = gate / (1.0 + jnp.exp(-gate)) * lift * weight
    ordered = [sums[first:first + count, :hidden] for first, count in pieces]
    middle = jnp.concatenate(ordered, axis=0).astype(jnp.bfloat16)
    own, near = shared_ref.shape[0] // CORES, near_ref.shape[0]
    for i in range(steps):
        at = slice(i * piece, (i + 1) * piece)
        term = jnp.dot(middle, down_ref[:, at], preferred_element_type=jnp.float32)
        shared = shared_ref[:, at]
        first = jnp.concatenate([term[:own] + shared[:own], term[own:rows]], axis=0)
        keep_ref[:, at] = first.astype(jnp.bfloat16)
        second = [term[rows:rows + own] + shared[own:], term[rows + own:rows + near]]
        near_ref[:, at] = jnp.concatenate(second, axis=0).astype(jnp.bfloat16)
        far_ref[:, at] = term[rows + near:].astype(jnp.bfloat16)


def routed_parts(gathered, flat, down, named, shared, pieces, near):
    count, width = sum(rows.shape[0] for rows in gathered), down.shape[1]
    half = count // CORES
    return pl.pallas_call(
        functools.partial(routed_kernel, pieces),
        in_specs=[pl.BlockSpec(memory_space=pltpu.VMEM)] * (len(gathered) + 4),
        out_specs=[pl.BlockSpec(memory_space=pltpu.VMEM)] * 3,
        out_shape=[jax.ShapeDtypeStruct((rows, width), jnp.bfloat16) for rows in (half, near, half - near)],
        scratch_shapes=[pltpu.VMEM((count, flat.shape[1]), jnp.float32)],
        compiler_params=pltpu.CompilerParams(vmem_limit_bytes=VMEM_LIMIT),
        cost_estimate=pl.CostEstimate(
            flops=2 * count * (flat.size + down.size),
            bytes_accessed=2 * (flat.size + down.size),
            transcendentals=0,
        ),
    )(*gathered, flat, down, named, shared)


def after(value, ready):
    return lax.optimization_barrier((value, ready))[0]


def exchange(rows, axis, flip):
    size = lax.axis_size(axis)
    return lax.ppermute(rows, axis, [(i, i ^ flip) for i in range(size)])


def half_ep(rows, experts):
    parts = [exchange(rows, "ep", chip) for chip in range(CORES, experts, CORES)]
    return jnp.concatenate([rows] + parts, axis=0)


def chip_sum(pair, experts, earlier=None):
    count = pair.shape[0] * CORES // experts
    total = pair[:count].astype(jnp.float32)
    for chip in range(CORES, experts, CORES):
        at = chip // CORES * count
        other = exchange(pair[at:at + count], "ep", chip)
        if earlier is not None:
            other = after(other, earlier)
        total = total + other.astype(jnp.float32)
    return total


def per_device(tokens, routes, gates, expert_up, expert_down, shared_up, shared_down):
    count, width = tokens.shape
    experts = lax.axis_size("ep")
    subs = lax.axis_size("sub")
    me = lax.axis_index("ep")
    bf = jnp.bfloat16

    lanes = -(-experts // LANES) * LANES
    named = (lax.broadcasted_iota(jnp.int32, (1, lanes), 1) == me).astype(jnp.float32)
    routed_rows = owner_rows(tokens, routes, gates, named, lanes)
    token_half = half_ep(after(tokens, routed_rows), experts)

    order = list(range(subs - 1, 1, -1))
    far = jnp.concatenate([exchange(routed_rows, "sub", k) for k in order], axis=0)
    own_half = half_ep(routed_rows, experts)
    near_half = exchange(own_half, "sub", 1)
    token_all = jnp.concatenate([token_half, exchange(token_half, "ep", 1)], axis=0)
    expert_weights, early = flat_pairs(expert_up[0], shared_up, routed_rows)
    far, expert_weights, _ = lax.optimization_barrier((far, expert_weights, token_half))
    middle = shared_middle(token_all, early, shared_up, far)

    far_chips = [exchange(after(far, own_half), "ep", chip) for chip in range(CORES, experts, CORES)]
    first = jnp.concatenate([own_half, far], axis=0)
    late = after(jnp.concatenate([near_half] + far_chips, axis=0), middle)
    gathered = (first, late, exchange(first, "ep", 1), exchange(late, "ep", 1))

    chips, split = experts // CORES, own_half.shape[0]
    pieces = []
    for core in range(CORES):
        at_first = core * (first.shape[0] + late.shape[0])
        at_late = at_first + first.shape[0]
        pieces += [(at_first, split), (at_late, split)]
        for at in reversed(range(len(order))):
            pieces.append((at_first + split + at * count, count))
            pieces += [
                (at_late + split + (chip * len(order) + at) * count, count) for chip in range(chips - 1)
            ]
    shared_part = jnp.dot(middle, shared_down, preferred_element_type=jnp.float32)
    keep, send_near, send_far = routed_parts(
        gathered, expert_weights, expert_down[0], named, shared_part, pieces, 2 * split
    )

    def pair_sum(own, send):
        return (own.astype(jnp.float32) + exchange(send, "ep", 1).astype(jnp.float32)).astype(bf)

    pair = pair_sum(keep[2 * split:], send_far)
    sums = []
    for at in range(0, pair.shape[0], split):
        earlier = sums[-1] if sums else None
        sums.append(chip_sum(pair[at:at + split], experts, earlier).astype(bf))
    pair = pair_sum(keep[:2 * split], send_near)
    near = exchange(pair[split:], "sub", 1)
    near = (pair[:split].astype(jnp.float32) + near.astype(jnp.float32)).astype(bf)
    total = chip_sum(near, experts)
    for rows, k in zip(sums, order[::-1]):
        total = total + exchange(rows, "sub", k).astype(jnp.float32)
    return total.astype(bf)


def solution(mesh):
    return jax.shard_map(
        per_device,
        mesh=mesh,
        in_specs=(
            P(("groups", "ep", "sub"), None),
            P(("groups", "ep", "sub"), None),
            P(("groups", "ep", "sub"), None),
            P("ep", None, None, "sub"),
            P("ep", "sub", None),
            P(None, None, "ep"),
            P("ep", None),
        ),
        out_specs=P(("groups", "ep", "sub"), None),
        check_vma=False,
    )
```
